32 devices in a mesh: sys: 8 (over z, y), mode: 2 (over x), rank: 2 (over core).
Axes of the slice: x: 2, y: 2, z: 4, core: 2. Of those that a mesh axis runs over, the one named last changes fastest.
Arguments:
- solution_core: bfloat16 [512, 256, 64], P(('sys', 'rank'), 'mode'), parts along dimension 0, may hold values from -6 to 6
- operator_core: bfloat16 [64, 256, 256, 8], P('sys', 'rank', 'mode'), parts along dimension 0, may hold values from -0.125 to 0.125
- left_interface: bfloat16 [512, 8, 64], P('sys', None, 'rank'), parts along dimension 0, may hold values from -0.25 to 0.25
- right_interface: bfloat16 [512, 8, 16], P('sys'), parts along dimension 0, may hold values from -0.75 to 0.75
- rhs_left: bfloat16 [512, 16], P(('sys', 'rank')), parts along dimension 0, may hold values from -1.5 to 1.5
- rhs_core: bfloat16 [128, 256, 16], P('sys', 'mode'), parts along dimension 0, may hold values from -6 to 6
- rhs_right: bfloat16 [128, 16], P('sys'), parts along dimension 0, may hold values from -1.5 to 1.5
Outputs:
- q_core: float32 [512, 256, 80], P(('sys', 'rank'), 'mode'), parts along dimension 0
- r_factor: float32 [640, 80], P('sys'), parts along dimension 0
The draws below stay inside these ranges and needn't reach their ends.
There are 8 independent parts, one for each index of `sys`. The reference program is written for one: setup_inputs(seed, part) draws one part's arguments, and reference() takes and returns one part's arrays. A program takes and returns all parts, laid end to end along the dimension named above; each array names one. Nothing has to cross between parts.
All inputs are finite; a program needn't handle non-finite values.
Results may differ from the reference program's by a relative error of at most 0.0014.
Values may be sent and summed in bfloat16 or wider, within the bound.
A program may use at most 64 MiB of HBM per device.

```python
import jax
import jax.numpy as jnp
from jax import lax

R = 64
MODE = 256
RA = 8
RZ = 16
RF = 16
N_MODE = 2


def steps_of(rng, dims, split, least, largest):
    loudness = 1.0
    for dim, blocks in split:
        draws = jax.random.uniform(jax.random.fold_in(jax.random.fold_in(rng, 6), dim), (blocks,), jnp.float32, least / len(split), largest / len(split))
        loudness = loudness * jnp.repeat(jnp.exp(draws), dims[dim] // blocks).reshape((-1,) + (1,) * (len(dims) - 1 - dim))
    return loudness


def normal_values(key, extent, scale, bound, shards=(), held_as=jnp.bfloat16):
    values = jax.random.normal(key, extent, jnp.float32) * scale
    if len(shards) > 0:
        values = steps_of(key, extent, shards, -0.22, 0.18) * values
    return jnp.clip(values, min=-bound, max=bound).astype(held_as)


def setup_inputs(seed: int = 0, part: int = 0) -> dict:
    streams_of = jax.random.split(jax.random.key(seed), 8)
    own_keys = jax.random.split(jax.random.fold_in(streams_of[7], part), 8)
    return {
        "solution_core": normal_values(own_keys[0], (R, MODE, R), 1.0, 6.0, ((0, 2), (1, 2))),
        "operator_core": normal_values(own_keys[1], (RA, MODE, MODE, RA), (MODE * RA) ** -0.5, 0.125, ((1, 2), (2, 2))),
        "left_interface": normal_values(own_keys[2], (R, RA, R), (R * RA) ** -0.5, 0.25, ((2, 2),)),
        "right_interface": normal_values(own_keys[3], (R, RA, RZ), R ** -0.5, 0.75),
        "rhs_left": normal_values(own_keys[4], (R, RF), RF ** -0.5, 1.5, ((0, 2),)),
        "rhs_core": normal_values(own_keys[5], (RF, MODE, RF), 1.0, 6.0, ((1, 2),)),
        "rhs_right": normal_values(own_keys[6], (RF, RZ), RF ** -0.5, 1.5),
    }


def reference(solution_core, operator_core, left_interface, right_interface, rhs_left, rhs_core, rhs_right):
    f32 = jnp.float32
    projected = jnp.einsum('cjd,dyb->cjyb', solution_core.astype(f32), right_interface.astype(f32)).astype(jnp.bfloat16)
    width = MODE // N_MODE
    operator_term = jnp.zeros((R, MODE, RZ), f32)
    for block in range(N_MODE):
        ops = operator_core[:, :, block * width:(block + 1) * width, :].astype(f32)
        proj = projected[:, block * width:(block + 1) * width].astype(f32)
        applied = jnp.einsum('xijy,cjyb->cxib', ops, proj).astype(jnp.bfloat16)
        operator_term = operator_term + jnp.einsum('axc,cxib->aib', left_interface.astype(f32), applied.astype(f32))
    rhs_term = jnp.einsum('af,fig,gb->aib', rhs_left.astype(f32), rhs_core.astype(f32), rhs_right.astype(f32), precision=lax.Precision.HIGHEST)
    residual_core = rhs_term - operator_term
    enriched = jnp.concatenate([solution_core.astype(f32), residual_core], axis=2).reshape(R * MODE, R + RZ)
    gram = jnp.dot(enriched.T, enriched, precision=lax.Precision.HIGHEST)
    lower = jnp.linalg.cholesky(gram)
    solved = lax.linalg.triangular_solve(lower, enriched, left_side=False, lower=True, transpose_a=True)
    q_core = solved.reshape(R, MODE, R + RZ)
    return (q_core, lower.T)
```

```python
import functools

import jax
import jax.numpy as jnp
from jax import lax
from jax.experimental import pallas as pl
from jax.experimental.pallas import tpu as pltpu
from jax.sharding import PartitionSpec as P

F32 = jnp.float32
BF16 = jnp.bfloat16
MESH = pl.DeviceIdType.MESH
NT = (((1,), (1,)), ((), ()))


def mm(a, b):
    return jnp.dot(a, b, preferred_element_type=F32)


def mm_nt(a, b):
    return lax.dot_general(a, b, NT, preferred_element_type=F32)


def iota(shape, dim):
    return lax.broadcasted_iota(jnp.int32, shape, dim)


def one_hot(cond):
    return jnp.where(cond, 1.0, 0.0).astype(BF16)


def turn(rows, inner, outer):
    row, col = iota((rows, rows), 0), iota((rows, rows), 1)
    return one_hot(col == (row % outer) * inner + row // outer)


def split2(x):
    hi = x.astype(BF16)
    return hi, (x - hi.astype(F32)).astype(BF16)


def term_kernel(
    dims,
    s_hbm, op_hbm, l_hbm, ri_ref, rl_ref, rc_ref, rr_ref,
    res_ref, gram_ref,
    s_all, l_all, op_raw, op2, pblk, z_ref, a_ref, t_ref, tb_ref, t_recv, g_all,
    loc_sem, s_send, s_recv, l_send, l_recv, t_send, t_rsem, g_send, g_recv,
):
    M, R, C, D, J, X, I, Y, A, B, F, G = dims
    m, r = lax.axis_index("mode"), lax.axis_index("rank")
    CT = C * R
    K = D + B

    def others(f):
        for mm_ in range(M):
            for rr_ in range(R):
                pl.when(jnp.logical_not((mm_ == m) & (rr_ == r)))(functools.partial(f, mm_, rr_))

    barrier = pltpu.get_barrier_semaphore()

    def greet(mm_, rr_):
        pl.semaphore_signal(barrier, inc=1, device_id={"mode": mm_, "rank": rr_}, device_id_type=MESH)

    others(greet)
    cp_s = pltpu.make_async_copy(s_hbm, s_all.at[r], loc_sem.at[0])
    cp_l = pltpu.make_async_copy(l_hbm, l_all.at[r], loc_sem.at[1])
    cp_o = pltpu.make_async_copy(op_hbm, op_raw, loc_sem.at[2])
    cp_s.start()
    cp_l.start()
    cp_o.start()
    cp_s.wait()
    cp_l.wait()
    pl.semaphore_wait(barrier, M * R - 1)

    def s_copy(rr_):
        return pltpu.make_async_remote_copy(
            src_ref=s_all.at[r], dst_ref=s_all.at[r], send_sem=s_send.at[rr_], recv_sem=s_recv.at[r],
            device_id={"rank": rr_}, device_id_type=MESH)

    def l_copy(rr_):
        return pltpu.make_async_remote_copy(
            src_ref=l_all.at[r], dst_ref=l_all.at[r], send_sem=l_send.at[rr_], recv_sem=l_recv.at[r],
            device_id={"rank": rr_}, device_id_type=MESH)

    def over_rank(f):
        for rr_ in range(R):
            pl.when(rr_ != r)(functools.partial(f, rr_))

    def start_sl(rr_):
        s_copy(rr_).start()
        l_copy(rr_).start()

    over_rank(start_sl)

    cp_o.wait()
    group = 2 * 128 // Y
    per = 256 // Y
    perm_op = turn(256, Y, per)

    def op_step(g, carry):
        both = jnp.concatenate(
            [op_raw[pl.ds(pl.multiple_of(g * 512, 512), 256), :],
             op_raw[pl.ds(pl.multiple_of(g * 512 + 256, 256), 256), :]], axis=1)
        out = mm(perm_op, both).astype(BF16)
        for h in range(2):
            for y in range(Y):
                op2[pl.ds(pl.multiple_of(g * 2 * per + h * per, per), per), y * J:(y + 1) * J] = (
                    out[y * per:(y + 1) * per, h * J:(h + 1) * J])
        return carry

    lax.fori_loop(0, X * I * Y // 512, op_step, 0, unroll=4)

    AB, FG = C * B, F * G
    row_ab, col_fg = iota((AB, 1), 0), iota((1, FG), 1)
    pick_a = one_hot(row_ab // B == iota((AB, C), 1))
    pick_b = one_hot(row_ab % B == iota((AB, B), 1))
    pick_f = one_hot(iota((F, FG), 0) == col_fg // G)
    pick_g = one_hot(iota((G, FG), 0) == col_fg % G)
    left = mm(mm_nt(pick_a, rl_ref[...]).astype(BF16), pick_f)
    right = mm(mm_nt(pick_b, rr_ref[...]).astype(BF16), pick_g)
    k_hi, k_lo = split2(left * right)
    rc = rc_ref[...]
    res_ref[...] = mm(k_hi, rc) + mm(k_lo, rc)

    ri_t = ri_ref[...]
    perm_cb = turn(16 * B, B, 16)

    def project(rr_):
        for cg in range(C // 16):
            for c2 in range(8):
                c = cg * 16 + c2 * 2
                both = jnp.concatenate(
                    [s_all[rr_, c * D:(c + 1) * D, :], s_all[rr_, (c + 1) * D:(c + 2) * D, :]], axis=1)
                p = mm(ri_t, both).astype(BF16)
                for h in range(2):
                    for y in range(Y):
                        pblk[(c2 * 2 + h) * B:(c2 * 2 + h + 1) * B, y * J:(y + 1) * J] = (
                            p[y * B:(y + 1) * B, h * J:(h + 1) * J])
            zz = mm(perm_cb, pblk[...]).astype(BF16)
            for b in range(B):
                row = pl.multiple_of(b * CT + rr_ * C + cg * 16, 16)
                z_ref[pl.ds(row, 16), :] = zz[b * 16:(b + 1) * 16, :]

    project(r)

    def wait_sl(rr_):
        cp = s_copy(rr_)
        pltpu.make_async_remote_copy(
            src_ref=s_all.at[rr_], dst_ref=s_all.at[rr_], send_sem=s_send.at[rr_], recv_sem=s_recv.at[rr_],
            device_id={"rank": rr_}, device_id_type=MESH).wait_recv()
        pltpu.make_async_remote_copy(
            src_ref=l_all.at[rr_], dst_ref=l_all.at[rr_], send_sem=l_send.at[rr_], recv_sem=l_recv.at[rr_],
            device_id={"rank": rr_}, device_id_type=MESH).wait_recv()
        cp.wait_send()
        l_copy(rr_).wait_send()

    over_rank(wait_sl)
    for k in range(1, R):
        project(lax.rem(r + k, R))

    def main_step(x2, carry):
        w = op2[pl.ds(pl.multiple_of(x2 * 2 * I, 2 * I), 2 * I), :]
        a_ref[x2] = mm_nt(z_ref[...], w).astype(BF16)
        return carry

    lax.fori_loop(0, X // 2, main_step, 0)

    l2 = jnp.concatenate([l_all[rr_] for rr_ in range(R)], axis=0).astype(F32).T.astype(BF16)
    for b2 in range(B // 2):
        cols = []
        for h in range(2):
            b = b2 * 2 + h
            cols.append(jnp.concatenate(
                [a_ref[x // 2, b * CT + rr_ * C:b * CT + (rr_ + 1) * C, (x % 2) * I:(x % 2 + 1) * I]
                 for rr_ in range(R) for x in range(X)], axis=0))
        t = mm(l2, jnp.concatenate(cols, axis=1))
        for h in range(2):
            t_ref[pl.ds(b2 * 2 + h, A, stride=B), :] = t[:, h * I:(h + 1) * I]
    tb_ref[...] = t_ref[...].astype(BF16)

    local = m == r

    def t_copy(rr_):
        return pltpu.make_async_remote_copy(
            src_ref=tb_ref.at[pl.ds(rr_ * AB, AB)], dst_ref=t_recv.at[m],
            send_sem=t_send.at[rr_], recv_sem=t_rsem.at[m],
            device_id={"mode": r, "rank": rr_}, device_id_type=MESH)

    for rr_ in range(R):
        pl.when(jnp.logical_not(local & (rr_ == r)))(lambda rr_=rr_: t_copy(rr_).start())

    @pl.when(local)
    def _():
        res_ref[...] -= t_ref[pl.ds(pl.multiple_of(r * AB, AB), AB), :]

    for mm_ in range(M):
        @pl.when(jnp.logical_not(local & (mm_ == m)))
        def _():
            pltpu.make_async_remote_copy(
                src_ref=tb_ref.at[pl.ds(0, AB)], dst_ref=t_recv.at[mm_],
                send_sem=t_send.at[0], recv_sem=t_rsem.at[mm_],
                device_id={"mode": r, "rank": 0}, device_id_type=MESH).wait_recv()
            res_ref[...] -= t_recv[mm_].astype(F32)

    hi, lo = split2(res_ref[...])
    g = jnp.zeros((D + 2 * B, D + 2 * B), F32)
    for a2 in range(C // 2):
        e = jnp.concatenate(
            [jnp.concatenate([s_all[r, a * D:(a + 1) * D, :], hi[a * B:(a + 1) * B], lo[a * B:(a + 1) * B]], axis=0)
             for a in (2 * a2, 2 * a2 + 1)], axis=1)
        g = g + mm_nt(e, e)
    g = jnp.concatenate([g[:D], g[D:K] + g[K:]], axis=0)
    g = jnp.concatenate([g[:, :D], g[:, D:K] + g[:, K:], jnp.zeros((K, 128 - K), F32)], axis=1)
    me = m * R + r
    g_all[me] = g

    def g_copy(mm_, rr_):
        return pltpu.make_async_remote_copy(
            src_ref=g_all.at[me], dst_ref=g_all.at[me],
            send_sem=g_send.at[mm_ * R + rr_], recv_sem=g_recv.at[me],
            device_id={"mode": mm_, "rank": rr_}, device_id_type=MESH)

    others(lambda mm_, rr_: g_copy(mm_, rr_).start())

    def g_wait(mm_, rr_):
        who = mm_ * R + rr_
        pltpu.make_async_remote_copy(
            src_ref=g_all.at[who], dst_ref=g_all.at[who], send_sem=g_send.at[who], recv_sem=g_recv.at[who],
            device_id={"mode": mm_, "rank": rr_}, device_id_type=MESH).wait_recv()

    others(g_wait)
    total = g_all[0]
    for who in range(1, M * R):
        total = total + g_all[who]
    gram_ref[...] = total
    others(lambda mm_, rr_: g_copy(mm_, rr_).wait_send())
    for rr_ in range(R):
        pl.when(jnp.logical_not(local & (rr_ == r)))(lambda rr_=rr_: t_copy(rr_).wait_send())


def eliminate(rows, n):
    sub = iota((8, 128), 0)
    done = [[None] * 8 for _ in rows]
    rows = [list(x) for x in rows]
    for k in range(n):
        kb, ks = divmod(k, 8)
        ga, ia = rows[kb]
        pivot = ga[ks:ks + 1, k:k + 1]
        inv = lax.rsqrt(pivot)
        grow, irow = ga[ks:ks + 1, :] * inv, ia[ks:ks + 1, :] * inv
        done[kb][ks] = (grow, irow)
        for q in range(kb, len(rows)):
            col = rows[q][0][:, k:k + 1] * inv
            rows[q] = [rows[q][0] - col * grow, rows[q][1] - col * irow]
    return done


def factor_kernel(dims, s_ref, res_ref, gram_ref, q_ref, r_ref):
    M, R, C, D, J, X, I, Y, A, B, F, G = dims
    K = D + B
    eye_row, eye_col = iota((8, 128), 0), iota((8, 128), 1)
    rows = [[gram_ref[8 * q:8 * q + 8, :], jnp.where(eye_col == eye_row + 8 * q, 1.0, 0.0)] for q in range(K // 8)]
    done = eliminate(rows, K)
    upper = jnp.concatenate([x[0] for blk in done for x in blk], axis=0)[:, :K]
    w = jnp.concatenate([x[1] for blk in done for x in blk], axis=0)[:, :K]
    tri = iota((K, K), 1) >= iota((K, K), 0)
    r_ref[...] = jnp.where(tri, upper, 0.0)
    w_hi, w_lo = split2(w)
    lhs = jnp.concatenate([w_hi, w_hi[:, D:], w_lo], axis=1)
    hi, lo = split2(res_ref[...])
    for a2 in range(C // 2):
        cols = []
        for a in (2 * a2, 2 * a2 + 1):
            s, h = s_ref[a * D:(a + 1) * D, :], hi[a * B:(a + 1) * B]
            cols.append(jnp.concatenate([s, h, lo[a * B:(a + 1) * B], s, h], axis=0))
        q = mm(lhs, jnp.concatenate(cols, axis=1))
        q_ref[2 * a2] = q[:, :I]
        q_ref[2 * a2 + 1] = q[:, I:]


def fused(n_mode, n_rank, solution_core, operator_core, left_interface, right_interface, rhs_left, rhs_core, rhs_right):
    C, J, D = solution_core.shape
    X, I, _, Y = operator_core.shape
    A = left_interface.shape[0]
    B = right_interface.shape[2]
    F, _, G = rhs_core.shape
    M, R = n_mode, n_rank
    dims = (M, R, C, D, J, X, I, Y, A, B, F, G)
    K = D + B
    s = solution_core.transpose(0, 2, 1).reshape(C * D, J)
    op = operator_core.transpose(0, 1, 3, 2).reshape(X * I * Y, J)
    li = left_interface.transpose(1, 2, 0).reshape(X * C, A)
    ri = right_interface.transpose(1, 2, 0).reshape(Y * B, D)
    rc = rhs_core.transpose(0, 2, 1).reshape(F * G, I)
    vmem = pl.BlockSpec(memory_space=pltpu.VMEM)
    hbm = pl.BlockSpec(memory_space=pl.ANY)
    DMA = pltpu.SemaphoreType.DMA
    res, gram = pl.pallas_call(
        functools.partial(term_kernel, dims),
        out_shape=(jax.ShapeDtypeStruct((C * B, I), F32), jax.ShapeDtypeStruct((K, 128), F32)),
        in_specs=[hbm, hbm, hbm, vmem, vmem, vmem, vmem],
        out_specs=(vmem, vmem),
        scratch_shapes=[
            pltpu.VMEM((R, C * D, J), BF16),
            pltpu.VMEM((R, X * C, A), BF16),
            pltpu.VMEM((X * I * Y, J), BF16),
            pltpu.VMEM((X * I, Y * J), BF16),
            pltpu.VMEM((16 * B, Y * J), BF16),
            pltpu.VMEM((B * C * R, Y * J), BF16),
            pltpu.VMEM((X // 2, B * C * R, 2 * I), BF16),
            pltpu.VMEM((A * B, I), F32),
            pltpu.VMEM((A * B, I), BF16),
            pltpu.VMEM((M, C * B, I), BF16),
            pltpu.VMEM((M * R, K, 128), F32),
            DMA((3,)), DMA((R,)), DMA((R,)), DMA((R,)), DMA((R,)),
            DMA((R,)), DMA((M,)), DMA((M * R,)), DMA((M * R,)),
        ],
        compiler_params=pltpu.CompilerParams(
            collective_id=0, has_side_effects=True, vmem_limit_bytes=48 * 1024 * 1024),
    )(s, op, li, ri, rhs_left.T, rc, rhs_right)
    q, r_factor = pl.pallas_call(
        functools.partial(factor_kernel, dims),
        out_shape=(jax.ShapeDtypeStruct((C, K, I), F32), jax.ShapeDtypeStruct((K, K), F32)),
        in_specs=[vmem, vmem, vmem],
        out_specs=(vmem, vmem),
        compiler_params=pltpu.CompilerParams(vmem_limit_bytes=48 * 1024 * 1024),
    )(s, res, gram)
    return q.transpose(0, 2, 1), r_factor


def plain(
    n_mode, n_rank, solution_core, operator_core, left_interface, right_interface, rhs_left, rhs_core, rhs_right
):
    highest = lax.Precision.HIGHEST
    left_rows, mode_rows, rank_full = solution_core.shape
    resid_rank = right_interface.shape[2]
    core_flat = solution_core.astype(F32).reshape(left_rows * mode_rows, rank_full)
    projected = jnp.einsum(
        "cjd,dyb->cjyb", solution_core, right_interface, preferred_element_type=F32
    ).astype(BF16)
    inter_turned = jnp.transpose(left_interface, (2, 1, 0))
    proj_piece = lax.all_gather(projected, "rank", axis=0, tiled=True)
    inter_piece = lax.all_gather(inter_turned, "rank", axis=0, tiled=True)
    applied = jnp.einsum(
        "xijy,cjyb->cxib", operator_core, proj_piece, preferred_element_type=F32
    ).astype(BF16)
    partial_value = jnp.einsum("cxa,cxib->aib", inter_piece, applied, preferred_element_type=F32)
    turned = lax.all_to_all(partial_value, "rank", split_axis=0, concat_axis=1, tiled=True)
    summed = lax.psum_scatter(turned, "mode", scatter_dimension=1, tiled=True)
    rhs_term = jnp.einsum(
        "af,fig,gb->aib",
        rhs_left.astype(F32),
        rhs_core.astype(F32),
        rhs_right.astype(F32),
        precision=highest,
    )
    residual_core = rhs_term - summed
    resid_flat = residual_core.reshape(left_rows * mode_rows, resid_rank)
    enriched = jnp.concatenate([core_flat, resid_flat], axis=1)
    gram = lax.psum(jnp.dot(enriched.T, enriched, precision=highest), ("mode", "rank"))
    lower = jnp.linalg.cholesky(gram)
    solved = lax.linalg.triangular_solve(
        lower, enriched, left_side=False, lower=True, transpose_a=True
    )
    q_core = solved.reshape(left_rows, mode_rows, rank_full + resid_rank)
    return (q_core, lower.T)


def per_device(n_mode, n_rank, *args):
    solution_core, operator_core, _, right_interface, _, rhs_core, _ = args
    C, J, D = solution_core.shape
    X, I, _, Y = operator_core.shape
    B = right_interface.shape[2]
    tiles = (
        n_mode == n_rank and J == 128 and I == 128 and rhs_core.shape[1] == I
        and C % 16 == 0 and B == 16 and D % 16 == 0 and D + B <= 128
        and 256 % Y == 0 and (256 // Y) % 16 == 0 and X % 2 == 0
    )
    return (fused if tiles else plain)(n_mode, n_rank, *args)


def solution(mesh):
    in_specs = (
        P(("sys", "rank"), "mode", None),
        P("sys", "rank", "mode", None),
        P("sys", None, "rank"),
        P("sys", None, None),
        P(("sys", "rank"), None),
        P("sys", "mode", None),
        P("sys", None),
    )
    out_specs = (P(("sys", "rank"), "mode", None), P("sys", None))
    return jax.shard_map(
        functools.partial(per_device, mesh.shape["mode"], mesh.shape["rank"]),
        mesh=mesh, in_specs=in_specs, out_specs=out_specs, check_vma=False,
    )
```

```python
import functools

import jax
import jax.numpy as jnp
from jax import lax
from jax.experimental import pallas as pl
from jax.experimental.pallas import tpu as pltpu
from jax.sharding import PartitionSpec as P

F32 = jnp.float32
BF16 = jnp.bfloat16
MESH = pl.DeviceIdType.MESH
NT = (((1,), (1,)), ((), ()))


def mm(a, b):
    return jnp.dot(a, b, preferred_element_type=F32)


def mm_nt(a, b):
    return lax.dot_general(a, b, NT, preferred_element_type=F32)


def iota(shape, dim):
    return lax.broadcasted_iota(jnp.int32, shape, dim)


def one_hot(cond):
    return jnp.where(cond, 1.0, 0.0).astype(BF16)


def turn(rows, inner, outer):
    row, col = iota((rows, rows), 0), iota((rows, rows), 1)
    return one_hot(col == (row % outer) * inner + row // outer)


def split2(x):
    hi = x.astype(BF16)
    return hi, (x - hi.astype(F32)).astype(BF16)


def term_kernel(
    dims,
    s_hbm, op_hbm, l_hbm, ri_hbm, rl_hbm, rc_hbm, rr_hbm,
    res_ref, gram_ref,
    ri_ref, rl_ref, rc_ref, rr_ref, s_all, l_all, op_raw, op2, pblk, z_ref, a_ref, t_ref, tb_ref, t_recv, g_all,
    loc_sem, s_send, s_recv, l_send, l_recv, t_send, t_rsem, g_send, g_recv,
):
    M, R, C, D, J, X, I, Y, A, B, F, G = dims
    m, r = lax.axis_index("mode"), lax.axis_index("rank")
    CT = C * R
    K = D + B

    def others(f):
        for mm_ in range(M):
            for rr_ in range(R):
                pl.when(jnp.logical_not((mm_ == m) & (rr_ == r)))(functools.partial(f, mm_, rr_))

    barrier = pltpu.get_barrier_semaphore()

    def greet(mm_, rr_):
        pl.semaphore_signal(barrier, inc=1, device_id={"mode": mm_, "rank": rr_}, device_id_type=MESH)

    others(greet)
    cp_s = pltpu.make_async_copy(s_hbm, s_all.at[r], loc_sem.at[0])
    cp_l = pltpu.make_async_copy(l_hbm, l_all.at[r], loc_sem.at[1])
    cp_o = pltpu.make_async_copy(op_hbm, op_raw, loc_sem.at[2])
    small = [
        pltpu.make_async_copy(src, dst, loc_sem.at[3 + k])
        for k, (src, dst) in enumerate(
            ((ri_hbm, ri_ref), (rl_hbm, rl_ref), (rc_hbm, rc_ref), (rr_hbm, rr_ref)))
    ]
    cp_s.start()
    cp_l.start()
    cp_o.start()
    for cp in small:
        cp.start()
    cp_s.wait()
    cp_l.wait()
    pl.semaphore_wait(barrier, M * R - 1)

    def s_copy(rr_):
        return pltpu.make_async_remote_copy(
            src_ref=s_all.at[r], dst_ref=s_all.at[r], send_sem=s_send.at[rr_], recv_sem=s_recv.at[r],
            device_id={"rank": rr_}, device_id_type=MESH)

    def l_copy(rr_):
        return pltpu.make_async_remote_copy(
            src_ref=l_all.at[r], dst_ref=l_all.at[r], send_sem=l_send.at[rr_], recv_sem=l_recv.at[r],
            device_id={"rank": rr_}, device_id_type=MESH)

    def over_rank(f):
        for rr_ in range(R):
            pl.when(rr_ != r)(functools.partial(f, rr_))

    def start_sl(rr_):
        s_copy(rr_).start()
        l_copy(rr_).start()

    over_rank(start_sl)

    cp_o.wait()
    group = 2 * 128 // Y
    per = 256 // Y
    perm_op = turn(256, Y, per)

    def op_step(g, carry):
        both = jnp.concatenate(
            [op_raw[pl.ds(pl.multiple_of(g * 512, 512), 256), :],
             op_raw[pl.ds(pl.multiple_of(g * 512 + 256, 256), 256), :]], axis=1)
        out = mm(perm_op, both).astype(BF16)
        for h in range(2):
            for y in range(Y):
                op2[pl.ds(pl.multiple_of(g * 2 * per + h * per, per), per), y * J:(y + 1) * J] = (
                    out[y * per:(y + 1) * per, h * J:(h + 1) * J])
        return carry

    lax.fori_loop(0, X * I * Y // 512, op_step, 0, unroll=4)

    for cp in small:
        cp.wait()

    AB, FG = C * B, F * G
    row_ab, col_fg = iota((AB, 1), 0), iota((1, FG), 1)
    pick_a = one_hot(row_ab // B == iota((AB, C), 1))
    pick_b = one_hot(row_ab % B == iota((AB, B), 1))
    pick_f = one_hot(iota((F, FG), 0) == col_fg // G)
    pick_g = one_hot(iota((G, FG), 0) == col_fg % G)
    left = mm(mm_nt(pick_a, rl_ref[...]).astype(BF16), pick_f)
    right = mm(mm_nt(pick_b, rr_ref[...]).astype(BF16), pick_g)
    k_hi, k_lo = split2(left * right)
    rc = rc_ref[...]
    res_ref[...] = mm(k_hi, rc) + mm(k_lo, rc)

    ri_t = ri_ref[...]
    perm_cb = turn(16 * B, B, 16)

    def project(rr_):
        for cg in range(C // 16):
            for c2 in range(8):
                c = cg * 16 + c2 * 2
                both = jnp.concatenate(
                    [s_all[rr_, c * D:(c + 1) * D, :], s_all[rr_, (c + 1) * D:(c + 2) * D, :]], axis=1)
                p = mm(ri_t, both).astype(BF16)
                for h in range(2):
                    for y in range(Y):
                        pblk[(c2 * 2 + h) * B:(c2 * 2 + h + 1) * B, y * J:(y + 1) * J] = (
                            p[y * B:(y + 1) * B, h * J:(h + 1) * J])
            zz = mm(perm_cb, pblk[...]).astype(BF16)
            for b in range(B):
                row = pl.multiple_of(b * CT + rr_ * C + cg * 16, 16)
                z_ref[pl.ds(row, 16), :] = zz[b * 16:(b + 1) * 16, :]

    project(r)

    def wait_sl(rr_):
        cp = s_copy(rr_)
        pltpu.make_async_remote_copy(
            src_ref=s_all.at[rr_], dst_ref=s_all.at[rr_], send_sem=s_send.at[rr_], recv_sem=s_recv.at[rr_],
            device_id={"rank": rr_}, device_id_type=MESH).wait_recv()
        pltpu.make_async_remote_copy(
            src_ref=l_all.at[rr_], dst_ref=l_all.at[rr_], send_sem=l_send.at[rr_], recv_sem=l_recv.at[rr_],
            device_id={"rank": rr_}, device_id_type=MESH).wait_recv()
        cp.wait_send()
        l_copy(rr_).wait_send()

    over_rank(wait_sl)
    for k in range(1, R):
        project(lax.rem(r + k, R))

    def main_step(x2, carry):
        w = op2[pl.ds(pl.multiple_of(x2 * 2 * I, 2 * I), 2 * I), :]
        a_ref[x2] = mm_nt(z_ref[...], w).astype(BF16)
        return carry

    lax.fori_loop(0, X // 2, main_step, 0)

    l2 = jnp.concatenate([l_all[rr_] for rr_ in range(R)], axis=0).astype(F32).T.astype(BF16)
    for b2 in range(B // 2):
        cols = []
        for h in range(2):
            b = b2 * 2 + h
            cols.append(jnp.concatenate(
                [a_ref[x // 2, b * CT + rr_ * C:b * CT + (rr_ + 1) * C, (x % 2) * I:(x % 2 + 1) * I]
                 for rr_ in range(R) for x in range(X)], axis=0))
        t = mm(l2, jnp.concatenate(cols, axis=1))
        for h in range(2):
            t_ref[pl.ds(b2 * 2 + h, A, stride=B), :] = t[:, h * I:(h + 1) * I]
    tb_ref[...] = t_ref[...].astype(BF16)

    local = m == r

    def t_copy(rr_):
        return pltpu.make_async_remote_copy(
            src_ref=tb_ref.at[pl.ds(rr_ * AB, AB)], dst_ref=t_recv.at[m],
            send_sem=t_send.at[rr_], recv_sem=t_rsem.at[m],
            device_id={"mode": r, "rank": rr_}, device_id_type=MESH)

    for rr_ in range(R):
        pl.when(jnp.logical_not(local & (rr_ == r)))(lambda rr_=rr_: t_copy(rr_).start())

    @pl.when(local)
    def _():
        res_ref[...] -= t_ref[pl.ds(pl.multiple_of(r * AB, AB), AB), :]

    for mm_ in range(M):
        @pl.when(jnp.logical_not(local & (mm_ == m)))
        def _():
            pltpu.make_async_remote_copy(
                src_ref=tb_ref.at[pl.ds(0, AB)], dst_ref=t_recv.at[mm_],
                send_sem=t_send.at[0], recv_sem=t_rsem.at[mm_],
                device_id={"mode": r, "rank": 0}, device_id_type=MESH).wait_recv()
            res_ref[...] -= t_recv[mm_].astype(F32)

    hi, lo = split2(res_ref[...])
    g = jnp.zeros((D + 2 * B, D + 2 * B), F32)
    for a2 in range(C // 2):
        e = jnp.concatenate(
            [jnp.concatenate([s_all[r, a * D:(a + 1) * D, :], hi[a * B:(a + 1) * B], lo[a * B:(a + 1) * B]], axis=0)
             for a in (2 * a2, 2 * a2 + 1)], axis=1)
        g = g + mm_nt(e, e)
    g = jnp.concatenate([g[:D], g[D:K] + g[K:]], axis=0)
    g = jnp.concatenate([g[:, :D], g[:, D:K] + g[:, K:], jnp.zeros((K, 128 - K), F32)], axis=1)
    me = m * R + r
    g_all[me] = g

    def g_copy(mm_, rr_):
        return pltpu.make_async_remote_copy(
            src_ref=g_all.at[me], dst_ref=g_all.at[me],
            send_sem=g_send.at[mm_ * R + rr_], recv_sem=g_recv.at[me],
            device_id={"mode": mm_, "rank": rr_}, device_id_type=MESH)

    others(lambda mm_, rr_: g_copy(mm_, rr_).start())

    def g_wait(mm_, rr_):
        who = mm_ * R + rr_
        pltpu.make_async_remote_copy(
            src_ref=g_all.at[who], dst_ref=g_all.at[who], send_sem=g_send.at[who], recv_sem=g_recv.at[who],
            device_id={"mode": mm_, "rank": rr_}, device_id_type=MESH).wait_recv()

    others(g_wait)
    total = g_all[0]
    for who in range(1, M * R):
        total = total + g_all[who]
    gram_ref[...] = total
    others(lambda mm_, rr_: g_copy(mm_, rr_).wait_send())
    for rr_ in range(R):
        pl.when(jnp.logical_not(local & (rr_ == r)))(lambda rr_=rr_: t_copy(rr_).wait_send())


def eliminate(rows, n):
    sub = iota((8, 128), 0)
    done = [[None] * 8 for _ in rows]
    rows = [list(x) for x in rows]
    for k in range(n):
        kb, ks = divmod(k, 8)
        ga, ia = rows[kb]
        pivot = ga[ks:ks + 1, k:k + 1]
        inv = lax.rsqrt(pivot)
        grow, irow = ga[ks:ks + 1, :] * inv, ia[ks:ks + 1, :] * inv
        done[kb][ks] = (grow, irow)
        for q in range(kb, len(rows)):
            col = rows[q][0][:, k:k + 1] * inv
            rows[q] = [rows[q][0] - col * grow, rows[q][1] - col * irow]
    return done


def factor_kernel(dims, s_hbm, res_ref, gram_ref, q_ref, r_ref, s_ref, sem):
    M, R, C, D, J, X, I, Y, A, B, F, G = dims
    K = D + B
    cp = pltpu.make_async_copy(s_hbm, s_ref, sem)
    cp.start()
    eye_row, eye_col = iota((8, 128), 0), iota((8, 128), 1)
    rows = [[gram_ref[8 * q:8 * q + 8, :], jnp.where(eye_col == eye_row + 8 * q, 1.0, 0.0)] for q in range(K // 8)]
    done = eliminate(rows, K)
    upper = jnp.concatenate([x[0] for blk in done for x in blk], axis=0)[:, :K]
    w = jnp.concatenate([x[1] for blk in done for x in blk], axis=0)[:, :K]
    tri = iota((K, K), 1) >= iota((K, K), 0)
    r_ref[...] = jnp.where(tri, upper, 0.0)
    w_hi, w_lo = split2(w)
    lhs = jnp.concatenate([w_hi, w_hi[:, D:], w_lo], axis=1)
    hi, lo = split2(res_ref[...])
    cp.wait()
    for a2 in range(C // 2):
        cols = []
        for a in (2 * a2, 2 * a2 + 1):
            s, h = s_ref[a * D:(a + 1) * D, :], hi[a * B:(a + 1) * B]
            cols.append(jnp.concatenate([s, h, lo[a * B:(a + 1) * B], s, h], axis=0))
        q = mm(lhs, jnp.concatenate(cols, axis=1))
        q_ref[2 * a2] = q[:, :I]
        q_ref[2 * a2 + 1] = q[:, I:]


def fused(n_mode, n_rank, solution_core, operator_core, left_interface, right_interface, rhs_left, rhs_core, rhs_right):
    C, J, D = solution_core.shape
    X, I, _, Y = operator_core.shape
    A = left_interface.shape[0]
    B = right_interface.shape[2]
    F, _, G = rhs_core.shape
    M, R = n_mode, n_rank
    dims = (M, R, C, D, J, X, I, Y, A, B, F, G)
    K = D + B
    s = solution_core.transpose(0, 2, 1).reshape(C * D, J)
    op = operator_core.transpose(0, 1, 3, 2).reshape(X * I * Y, J)
    li = left_interface.transpose(1, 2, 0).reshape(X * C, A)
    ri = right_interface.transpose(1, 2, 0).reshape(Y * B, D)
    rc = rhs_core.transpose(0, 2, 1).reshape(F * G, I)
    rl = rhs_left.T
    vmem = pl.BlockSpec(memory_space=pltpu.VMEM)
    hbm = pl.BlockSpec(memory_space=pl.ANY)
    DMA = pltpu.SemaphoreType.DMA
    res, gram = pl.pallas_call(
        functools.partial(term_kernel, dims),
        out_shape=(jax.ShapeDtypeStruct((C * B, I), F32), jax.ShapeDtypeStruct((K, 128), F32)),
        in_specs=[hbm] * 7,
        out_specs=(vmem, vmem),
        scratch_shapes=[
            pltpu.VMEM(ri.shape, BF16),
            pltpu.VMEM(rl.shape, BF16),
            pltpu.VMEM(rc.shape, BF16),
            pltpu.VMEM(rhs_right.shape, BF16),
            pltpu.VMEM((R, C * D, J), BF16),
            pltpu.VMEM((R, X * C, A), BF16),
            pltpu.VMEM((X * I * Y, J), BF16),
            pltpu.VMEM((X * I, Y * J), BF16),
            pltpu.VMEM((16 * B, Y * J), BF16),
            pltpu.VMEM((B * C * R, Y * J), BF16),
            pltpu.VMEM((X // 2, B * C * R, 2 * I), BF16),
            pltpu.VMEM((A * B, I), F32),
            pltpu.VMEM((A * B, I), BF16),
            pltpu.VMEM((M, C * B, I), BF16),
            pltpu.VMEM((M * R, K, 128), F32),
            DMA((7,)), DMA((R,)), DMA((R,)), DMA((R,)), DMA((R,)),
            DMA((R,)), DMA((M,)), DMA((M * R,)), DMA((M * R,)),
        ],
        compiler_params=pltpu.CompilerParams(
            collective_id=0, has_side_effects=True, vmem_limit_bytes=62 * 1024 * 1024),
    )(s, op, li, ri, rl, rc, rhs_right)
    q, r_factor = pl.pallas_call(
        functools.partial(factor_kernel, dims),
        out_shape=(jax.ShapeDtypeStruct((C, K, I), F32), jax.ShapeDtypeStruct((K, K), F32)),
        in_specs=[hbm, vmem, vmem],
        out_specs=(vmem, vmem),
        scratch_shapes=[pltpu.VMEM(s.shape, BF16), DMA],
        compiler_params=pltpu.CompilerParams(vmem_limit_bytes=62 * 1024 * 1024),
    )(s, res, gram)
    return q.transpose(0, 2, 1), r_factor


def plain(
    n_mode, n_rank, solution_core, operator_core, left_interface, right_interface, rhs_left, rhs_core, rhs_right
):
    highest = lax.Precision.HIGHEST
    left_rows, mode_rows, rank_full = solution_core.shape
    resid_rank = right_interface.shape[2]
    core_flat = solution_core.astype(F32).reshape(left_rows * mode_rows, rank_full)
    projected = jnp.einsum(
        "cjd,dyb->cjyb", solution_core, right_interface, preferred_element_type=F32
    ).astype(BF16)
    inter_turned = jnp.transpose(left_interface, (2, 1, 0))
    proj_piece = lax.all_gather(projected, "rank", axis=0, tiled=True)
    inter_piece = lax.all_gather(inter_turned, "rank", axis=0, tiled=True)
    applied = jnp.einsum(
        "xijy,cjyb->cxib", operator_core, proj_piece, preferred_element_type=F32
    ).astype(BF16)
    partial_value = jnp.einsum("cxa,cxib->aib", inter_piece, applied, preferred_element_type=F32)
    turned = lax.all_to_all(partial_value, "rank", split_axis=0, concat_axis=1, tiled=True)
    summed = lax.psum_scatter(turned, "mode", scatter_dimension=1, tiled=True)
    rhs_term = jnp.einsum(
        "af,fig,gb->aib",
        rhs_left.astype(F32),
        rhs_core.astype(F32),
        rhs_right.astype(F32),
        precision=highest,
    )
    residual_core = rhs_term - summed
    resid_flat = residual_core.reshape(left_rows * mode_rows, resid_rank)
    enriched = jnp.concatenate([core_flat, resid_flat], axis=1)
    gram = lax.psum(jnp.dot(enriched.T, enriched, precision=highest), ("mode", "rank"))
    lower = jnp.linalg.cholesky(gram)
    solved = lax.linalg.triangular_solve(
        lower, enriched, left_side=False, lower=True, transpose_a=True
    )
    q_core = solved.reshape(left_rows, mode_rows, rank_full + resid_rank)
    return (q_core, lower.T)


def per_device(n_mode, n_rank, *args):
    solution_core, operator_core, _, right_interface, _, rhs_core, _ = args
    C, J, D = solution_core.shape
    X, I, _, Y = operator_core.shape
    B = right_interface.shape[2]
    tiles = (
        n_mode == n_rank and J == 128 and I == 128 and rhs_core.shape[1] == I
        and C % 16 == 0 and B == 16 and D % 16 == 0 and D + B <= 128
        and 256 % Y == 0 and (256 // Y) % 16 == 0 and X % 2 == 0
    )
    return (fused if tiles else plain)(n_mode, n_rank, *args)


def solution(mesh):
    in_specs = (
        P(("sys", "rank"), "mode", None),
        P("sys", "rank", "mode", None),
        P("sys", None, "rank"),
        P("sys", None, None),
        P(("sys", "rank"), None),
        P("sys", "mode", None),
        P("sys", None),
    )
    out_specs = (P(("sys", "rank"), "mode", None), P("sys", None))
    return jax.shard_map(
        functools.partial(per_device, mesh.shape["mode"], mesh.shape["rank"]),
        mesh=mesh, in_specs=in_specs, out_specs=out_specs, check_vma=False,
    )
```

```python
import functools

import jax
import jax.numpy as jnp
from jax import lax
from jax.experimental import pallas as pl
from jax.experimental.pallas import tpu as pltpu
from jax.sharding import PartitionSpec as P

F32 = jnp.float32
BF16 = jnp.bfloat16
MESH = pl.DeviceIdType.MESH
NT = (((1,), (1,)), ((), ()))


def mm(a, b):
    return jnp.dot(a, b, preferred_element_type=F32)


def mm_nt(a, b):
    return lax.dot_general(a, b, NT, preferred_element_type=F32)


def iota(shape, dim):
    return lax.broadcasted_iota(jnp.int32, shape, dim)


def one_hot(cond):
    return jnp.where(cond, 1.0, 0.0).astype(BF16)


def turn(rows, inner, outer):
    row, col = iota((rows, rows), 0), iota((rows, rows), 1)
    return one_hot(col == (row % outer) * inner + row // outer)


def split2(x):
    hi = x.astype(BF16)
    return hi, (x - hi.astype(F32)).astype(BF16)


def term_kernel(
    dims,
    s_hbm, op_hbm, l_hbm, ri_hbm, rl_hbm, rc_hbm, rr_hbm,
    res_ref, gram_ref, fac_ref,
    ri_ref, rl_ref, rc_ref, rr_ref, s_all, l_all, op_raw, op2, pblk, z_ref, a_ref, t_ref, tb_ref, t_recv, g_all, gs_all,
    loc_sem, s_send, s_recv, l_send, l_recv, t_send, t_rsem, g_send, g_recv, gs_send, gs_recv,
):
    M, R, C, D, J, X, I, Y, A, B, F, G = dims
    m, r = lax.axis_index("mode"), lax.axis_index("rank")
    CT = C * R
    K = D + B

    def others(f):
        for mm_ in range(M):
            for rr_ in range(R):
                pl.when(jnp.logical_not((mm_ == m) & (rr_ == r)))(functools.partial(f, mm_, rr_))

    barrier = pltpu.get_barrier_semaphore()

    def greet(mm_, rr_):
        pl.semaphore_signal(barrier, inc=1, device_id={"mode": mm_, "rank": rr_}, device_id_type=MESH)

    others(greet)
    cp_s = pltpu.make_async_copy(s_hbm, s_all.at[r], loc_sem.at[0])
    cp_l = pltpu.make_async_copy(l_hbm, l_all.at[r], loc_sem.at[1])
    cp_o = pltpu.make_async_copy(op_hbm, op_raw, loc_sem.at[2])
    small = [
        pltpu.make_async_copy(src, dst, loc_sem.at[3 + k])
        for k, (src, dst) in enumerate(
            ((ri_hbm, ri_ref), (rl_hbm, rl_ref), (rc_hbm, rc_ref), (rr_hbm, rr_ref)))
    ]
    cp_s.start()
    cp_l.start()
    cp_o.start()
    for cp in small:
        cp.start()
    cp_s.wait()
    cp_l.wait()
    pl.semaphore_wait(barrier, M * R - 1)

    def s_copy(rr_):
        return pltpu.make_async_remote_copy(
            src_ref=s_all.at[r], dst_ref=s_all.at[r], send_sem=s_send.at[rr_], recv_sem=s_recv.at[r],
            device_id={"rank": rr_}, device_id_type=MESH)

    def l_copy(rr_):
        return pltpu.make_async_remote_copy(
            src_ref=l_all.at[r], dst_ref=l_all.at[r], send_sem=l_send.at[rr_], recv_sem=l_recv.at[r],
            device_id={"rank": rr_}, device_id_type=MESH)

    def over_rank(f):
        for rr_ in range(R):
            pl.when(rr_ != r)(functools.partial(f, rr_))

    def start_sl(rr_):
        s_copy(rr_).start()
        l_copy(rr_).start()

    over_rank(start_sl)

    me = m * R + r
    gs = jnp.zeros((D, D), F32)
    for a2 in range(C // 2):
        e = jnp.concatenate([s_all[r, a * D:(a + 1) * D, :] for a in (2 * a2, 2 * a2 + 1)], axis=1)
        gs = gs + mm_nt(e, e)
    gs_all[me] = jnp.concatenate([gs, jnp.zeros((D, 128 - D), F32)], axis=1)

    def sums(buf, send, recv):
        def copy(who, mm_, rr_):
            return pltpu.make_async_remote_copy(
                src_ref=buf.at[who], dst_ref=buf.at[who],
                send_sem=send.at[mm_ * R + rr_], recv_sem=recv.at[who],
                device_id={"mode": mm_, "rank": rr_}, device_id_type=MESH)

        def start():
            others(lambda mm_, rr_: copy(me, mm_, rr_).start())

        def finish():
            others(lambda mm_, rr_: copy(mm_ * R + rr_, mm_, rr_).wait_recv())
            total = buf[0]
            for who in range(1, M * R):
                total = total + buf[who]
            return total

        def sent():
            others(lambda mm_, rr_: copy(me, mm_, rr_).wait_send())

        return start, finish, sent

    gs_start, gs_finish, gs_sent = sums(gs_all, gs_send, gs_recv)
    g_start, g_finish, g_sent = sums(g_all, g_send, g_recv)
    gs_start()

    cp_o.wait()
    group = 2 * 128 // Y
    per = 256 // Y
    perm_op = turn(256, Y, per)

    def op_step(g, carry):
        both = jnp.concatenate(
            [op_raw[pl.ds(pl.multiple_of(g * 512, 512), 256), :],
             op_raw[pl.ds(pl.multiple_of(g * 512 + 256, 256), 256), :]], axis=1)
        out = mm(perm_op, both).astype(BF16)
        for h in range(2):
            for y in range(Y):
                op2[pl.ds(pl.multiple_of(g * 2 * per + h * per, per), per), y * J:(y + 1) * J] = (
                    out[y * per:(y + 1) * per, h * J:(h + 1) * J])
        return carry

    lax.fori_loop(0, X * I * Y // 512, op_step, 0, unroll=4)

    for cp in small:
        cp.wait()

    AB, FG = C * B, F * G
    row_ab, col_fg = iota((AB, 1), 0), iota((1, FG), 1)
    pick_a = one_hot(row_ab // B == iota((AB, C), 1))
    pick_b = one_hot(row_ab % B == iota((AB, B), 1))
    pick_f = one_hot(iota((F, FG), 0) == col_fg // G)
    pick_g = one_hot(iota((G, FG), 0) == col_fg % G)
    left = mm(mm_nt(pick_a, rl_ref[...]).astype(BF16), pick_f)
    right = mm(mm_nt(pick_b, rr_ref[...]).astype(BF16), pick_g)
    k_hi, k_lo = split2(left * right)
    rc = rc_ref[...]
    res_ref[...] = mm(k_hi, rc) + mm(k_lo, rc)

    ri_t = ri_ref[...]
    perm_cb = turn(16 * B, B, 16)

    def project(rr_):
        for cg in range(C // 16):
            for c2 in range(8):
                c = cg * 16 + c2 * 2
                both = jnp.concatenate(
                    [s_all[rr_, c * D:(c + 1) * D, :], s_all[rr_, (c + 1) * D:(c + 2) * D, :]], axis=1)
                p = mm(ri_t, both).astype(BF16)
                for h in range(2):
                    for y in range(Y):
                        pblk[(c2 * 2 + h) * B:(c2 * 2 + h + 1) * B, y * J:(y + 1) * J] = (
                            p[y * B:(y + 1) * B, h * J:(h + 1) * J])
            zz = mm(perm_cb, pblk[...]).astype(BF16)
            for b in range(B):
                row = pl.multiple_of(b * CT + rr_ * C + cg * 16, 16)
                z_ref[pl.ds(row, 16), :] = zz[b * 16:(b + 1) * 16, :]

    project(r)

    def wait_sl(rr_):
        cp = s_copy(rr_)
        pltpu.make_async_remote_copy(
            src_ref=s_all.at[rr_], dst_ref=s_all.at[rr_], send_sem=s_send.at[rr_], recv_sem=s_recv.at[rr_],
            device_id={"rank": rr_}, device_id_type=MESH).wait_recv()
        pltpu.make_async_remote_copy(
            src_ref=l_all.at[rr_], dst_ref=l_all.at[rr_], send_sem=l_send.at[rr_], recv_sem=l_recv.at[rr_],
            device_id={"rank": rr_}, device_id_type=MESH).wait_recv()
        cp.wait_send()
        l_copy(rr_).wait_send()

    over_rank(wait_sl)
    for k in range(1, R):
        project(lax.rem(r + k, R))

    def main_step(x2, carry):
        w = op2[pl.ds(pl.multiple_of(x2 * 2 * I, 2 * I), 2 * I), :]
        a_ref[x2] = mm_nt(z_ref[...], w).astype(BF16)
        return carry

    lax.fori_loop(0, X // 2, main_step, 0)

    l2 = jnp.concatenate([l_all[rr_] for rr_ in range(R)], axis=0).astype(F32).T.astype(BF16)
    for b2 in range(B // 2):
        cols = []
        for h in range(2):
            b = b2 * 2 + h
            cols.append(jnp.concatenate(
                [a_ref[x // 2, b * CT + rr_ * C:b * CT + (rr_ + 1) * C, (x % 2) * I:(x % 2 + 1) * I]
                 for rr_ in range(R) for x in range(X)], axis=0))
        t = mm(l2, jnp.concatenate(cols, axis=1))
        for h in range(2):
            t_ref[pl.ds(b2 * 2 + h, A, stride=B), :] = t[:, h * I:(h + 1) * I]
    tb_ref[...] = t_ref[...].astype(BF16)

    local = m == r

    def t_copy(rr_):
        return pltpu.make_async_remote_copy(
            src_ref=tb_ref.at[pl.ds(rr_ * AB, AB)], dst_ref=t_recv.at[m],
            send_sem=t_send.at[rr_], recv_sem=t_rsem.at[m],
            device_id={"mode": r, "rank": rr_}, device_id_type=MESH)

    for rr_ in range(R):
        pl.when(jnp.logical_not(local & (rr_ == r)))(lambda rr_=rr_: t_copy(rr_).start())

    fac_ref[...] = eliminate(gs_finish(), D)

    @pl.when(local)
    def _():
        res_ref[...] -= t_ref[pl.ds(pl.multiple_of(r * AB, AB), AB), :]

    for mm_ in range(M):
        @pl.when(jnp.logical_not(local & (mm_ == m)))
        def _():
            pltpu.make_async_remote_copy(
                src_ref=tb_ref.at[pl.ds(0, AB)], dst_ref=t_recv.at[mm_],
                send_sem=t_send.at[0], recv_sem=t_rsem.at[mm_],
                device_id={"mode": r, "rank": 0}, device_id_type=MESH).wait_recv()
            res_ref[...] -= t_recv[mm_].astype(F32)

    hi, lo = split2(res_ref[...])
    g = jnp.zeros((2 * B, D + 2 * B), F32)
    for a2 in range(C // 2):
        hl = jnp.concatenate(
            [jnp.concatenate([hi[a * B:(a + 1) * B], lo[a * B:(a + 1) * B]], axis=0)
             for a in (2 * a2, 2 * a2 + 1)], axis=1)
        e = jnp.concatenate([s_all[r, a * D:(a + 1) * D, :] for a in (2 * a2, 2 * a2 + 1)], axis=1)
        g = g + mm_nt(hl, jnp.concatenate([e, hl], axis=0))
    g = g[:B] + g[B:]
    g_all[me] = jnp.concatenate([g[:, :D], g[:, D:K] + g[:, K:], jnp.zeros((B, 128 - K), F32)], axis=1)
    g_start()
    gram_ref[...] = g_finish()
    g_sent()
    gs_sent()
    for rr_ in range(R):
        pl.when(jnp.logical_not(local & (rr_ == r)))(lambda rr_=rr_: t_copy(rr_).wait_send())


def eliminate(gram, n):
    a = jnp.where(iota((n, 128), 1) == iota((n, 128), 0) + n, 1.0, gram)
    done = []
    for k in range(n):
        if k % 8 == 0 and k > 0:
            a = a[8:]
        ks = k % 8
        inv = lax.rsqrt(a[ks:ks + 1, k:k + 1])
        row = a[ks:ks + 1, :] * inv
        done.append(row)
        a = a - (a[:, k:k + 1] * inv) * row
    return jnp.concatenate(done, axis=0)


def factor_kernel(dims, s_hbm, res_ref, gram_ref, fac_ref, q_ref, r_ref, s_ref, sem):
    M, R, C, D, J, X, I, Y, A, B, F, G = dims
    K = D + B
    cp = pltpu.make_async_copy(s_hbm, s_ref, sem)
    cp.start()
    exact = functools.partial(lax.dot_general, precision=lax.Precision.HIGHEST, preferred_element_type=F32)
    NN = (((1,), (0,)), ((), ()))
    u11, w11 = fac_ref[:, :D], fac_ref[:, D:2 * D]
    g21 = gram_ref[:, :D]
    l21 = exact(g21, w11, NT)
    u12 = exact(w11, g21, NT)
    s22 = gram_ref[:, D:K] - exact(l21, l21, NT)
    last = eliminate(jnp.concatenate([s22, jnp.zeros((B, 128 - B), F32)], axis=1), B)
    u22, w22 = last[:, :B], last[:, B:2 * B]
    w21 = -exact(w22, exact(l21, w11, NN), NN)
    upper = jnp.concatenate(
        [jnp.concatenate([u11, u12], axis=1), jnp.concatenate([jnp.zeros((B, D), F32), u22], axis=1)], axis=0)
    w = jnp.concatenate(
        [jnp.concatenate([w11, jnp.zeros((D, B), F32)], axis=1), jnp.concatenate([w21, w22], axis=1)], axis=0)
    tri = iota((K, K), 1) >= iota((K, K), 0)
    r_ref[...] = jnp.where(tri, upper, 0.0)
    w_hi, w_lo = split2(w)
    lhs = jnp.concatenate([w_hi, w_hi[:, D:], w_lo], axis=1)
    hi, lo = split2(res_ref[...])
    cp.wait()
    for a2 in range(C // 2):
        cols = []
        for a in (2 * a2, 2 * a2 + 1):
            s, h = s_ref[a * D:(a + 1) * D, :], hi[a * B:(a + 1) * B]
            cols.append(jnp.concatenate([s, h, lo[a * B:(a + 1) * B], s, h], axis=0))
        q = mm(lhs, jnp.concatenate(cols, axis=1))
        q_ref[2 * a2] = q[:, :I]
        q_ref[2 * a2 + 1] = q[:, I:]


def fused(n_mode, n_rank, solution_core, operator_core, left_interface, right_interface, rhs_left, rhs_core, rhs_right):
    C, J, D = solution_core.shape
    X, I, _, Y = operator_core.shape
    A = left_interface.shape[0]
    B = right_interface.shape[2]
    F, _, G = rhs_core.shape
    M, R = n_mode, n_rank
    dims = (M, R, C, D, J, X, I, Y, A, B, F, G)
    K = D + B
    s = solution_core.transpose(0, 2, 1).reshape(C * D, J)
    op = operator_core.transpose(0, 1, 3, 2).reshape(X * I * Y, J)
    li = left_interface.transpose(1, 2, 0).reshape(X * C, A)
    ri = right_interface.transpose(1, 2, 0).reshape(Y * B, D)
    rc = rhs_core.transpose(0, 2, 1).reshape(F * G, I)
    rl = rhs_left.T
    vmem = pl.BlockSpec(memory_space=pltpu.VMEM)
    hbm = pl.BlockSpec(memory_space=pl.ANY)
    DMA = pltpu.SemaphoreType.DMA
    res, gram, fac = pl.pallas_call(
        functools.partial(term_kernel, dims),
        out_shape=(jax.ShapeDtypeStruct((C * B, I), F32), jax.ShapeDtypeStruct((B, 128), F32),
                   jax.ShapeDtypeStruct((D, 128), F32)),
        in_specs=[hbm] * 7,
        out_specs=(vmem, vmem, vmem),
        scratch_shapes=[
            pltpu.VMEM(ri.shape, BF16),
            pltpu.VMEM(rl.shape, BF16),
            pltpu.VMEM(rc.shape, BF16),
            pltpu.VMEM(rhs_right.shape, BF16),
            pltpu.VMEM((R, C * D, J), BF16),
            pltpu.VMEM((R, X * C, A), BF16),
            pltpu.VMEM((X * I * Y, J), BF16),
            pltpu.VMEM((X * I, Y * J), BF16),
            pltpu.VMEM((16 * B, Y * J), BF16),
            pltpu.VMEM((B * C * R, Y * J), BF16),
            pltpu.VMEM((X // 2, B * C * R, 2 * I), BF16),
            pltpu.VMEM((A * B, I), F32),
            pltpu.VMEM((A * B, I), BF16),
            pltpu.VMEM((M, C * B, I), BF16),
            pltpu.VMEM((M * R, B, 128), F32),
            pltpu.VMEM((M * R, D, 128), F32),
            DMA((7,)), DMA((R,)), DMA((R,)), DMA((R,)), DMA((R,)),
            DMA((R,)), DMA((M,)), DMA((M * R,)), DMA((M * R,)), DMA((M * R,)), DMA((M * R,)),
        ],
        compiler_params=pltpu.CompilerParams(
            collective_id=0, has_side_effects=True, vmem_limit_bytes=62 * 1024 * 1024),
    )(s, op, li, ri, rl, rc, rhs_right)
    q, r_factor = pl.pallas_call(
        functools.partial(factor_kernel, dims),
        out_shape=(jax.ShapeDtypeStruct((C, K, I), F32), jax.ShapeDtypeStruct((K, K), F32)),
        in_specs=[hbm, vmem, vmem, vmem],
        out_specs=(vmem, vmem),
        scratch_shapes=[pltpu.VMEM(s.shape, BF16), DMA],
        compiler_params=pltpu.CompilerParams(vmem_limit_bytes=62 * 1024 * 1024),
    )(s, res, gram, fac)
    return q.transpose(0, 2, 1), r_factor


def plain(
    n_mode, n_rank, solution_core, operator_core, left_interface, right_interface, rhs_left, rhs_core, rhs_right
):
    highest = lax.Precision.HIGHEST
    left_rows, mode_rows, rank_full = solution_core.shape
    resid_rank = right_interface.shape[2]
    core_flat = solution_core.astype(F32).reshape(left_rows * mode_rows, rank_full)
    projected = jnp.einsum(
        "cjd,dyb->cjyb", solution_core, right_interface, preferred_element_type=F32
    ).astype(BF16)
    inter_turned = jnp.transpose(left_interface, (2, 1, 0))
    proj_piece = lax.all_gather(projected, "rank", axis=0, tiled=True)
    inter_piece = lax.all_gather(inter_turned, "rank", axis=0, tiled=True)
    applied = jnp.einsum(
        "xijy,cjyb->cxib", operator_core, proj_piece, preferred_element_type=F32
    ).astype(BF16)
    partial_value = jnp.einsum("cxa,cxib->aib", inter_piece, applied, preferred_element_type=F32)
    turned = lax.all_to_all(partial_value, "rank", split_axis=0, concat_axis=1, tiled=True)
    summed = lax.psum_scatter(turned, "mode", scatter_dimension=1, tiled=True)
    rhs_term = jnp.einsum(
        "af,fig,gb->aib",
        rhs_left.astype(F32),
        rhs_core.astype(F32),
        rhs_right.astype(F32),
        precision=highest,
    )
    residual_core = rhs_term - summed
    resid_flat = residual_core.reshape(left_rows * mode_rows, resid_rank)
    enriched = jnp.concatenate([core_flat, resid_flat], axis=1)
    gram = lax.psum(jnp.dot(enriched.T, enriched, precision=highest), ("mode", "rank"))
    lower = jnp.linalg.cholesky(gram)
    solved = lax.linalg.triangular_solve(
        lower, enriched, left_side=False, lower=True, transpose_a=True
    )
    q_core = solved.reshape(left_rows, mode_rows, rank_full + resid_rank)
    return (q_core, lower.T)


def per_device(n_mode, n_rank, *args):
    solution_core, operator_core, _, right_interface, _, rhs_core, _ = args
    C, J, D = solution_core.shape
    X, I, _, Y = operator_core.shape
    B = right_interface.shape[2]
    tiles = (
        n_mode == n_rank and J == 128 and I == 128 and rhs_core.shape[1] == I
        and C % 16 == 0 and B == 16 and D % 16 == 0 and D + B <= 128 and 2 * D <= 128
        and 256 % Y == 0 and (256 // Y) % 16 == 0 and X % 2 == 0
    )
    return (fused if tiles else plain)(n_mode, n_rank, *args)


def solution(mesh):
    in_specs = (
        P(("sys", "rank"), "mode", None),
        P("sys", "rank", "mode", None),
        P("sys", None, "rank"),
        P("sys", None, None),
        P(("sys", "rank"), None),
        P("sys", "mode", None),
        P("sys", None),
    )
    out_specs = (P(("sys", "rank"), "mode", None), P("sys", None))
    return jax.shard_map(
        functools.partial(per_device, mesh.shape["mode"], mesh.shape["rank"]),
        mesh=mesh, in_specs=in_specs, out_specs=out_specs, check_vma=False,
    )
```

```python
import functools

import jax
import jax.numpy as jnp
from jax import lax
from jax.experimental import pallas as pl
from jax.experimental.pallas import tpu as pltpu
from jax.sharding import PartitionSpec as P

F32 = jnp.float32
BF16 = jnp.bfloat16
MESH = pl.DeviceIdType.MESH
NT = (((1,), (1,)), ((), ()))


def mm(a, b):
    return jnp.dot(a, b, preferred_element_type=F32)


def mm_nt(a, b):
    return lax.dot_general(a, b, NT, preferred_element_type=F32)


def iota(shape, dim):
    return lax.broadcasted_iota(jnp.int32, shape, dim)


def one_hot(cond):
    return jnp.where(cond, 1.0, 0.0).astype(BF16)


def turn(rows, inner, outer):
    row, col = iota((rows, rows), 0), iota((rows, rows), 1)
    return one_hot(col == (row % outer) * inner + row // outer)


def split2(x):
    hi = x.astype(BF16)
    return hi, (x - hi.astype(F32)).astype(BF16)


def term_kernel(
    dims,
    s_hbm, op_hbm, l_hbm, ri_hbm, rl_hbm, rc_hbm, rr_hbm,
    res_ref, gram_ref, fac_ref,
    ri_ref, rl_ref, rc_ref, rr_ref, s_all, l_all, op_raw, op2, pblk, z_ref, a_ref, t_ref, tb_ref, t_recv, g_all, gs_all,
    loc_sem, s_send, s_recv, l_send, l_recv, t_send, t_rsem, g_send, g_recv, gs_send, gs_recv,
):
    M, R, C, D, J, X, I, Y, A, B, F, G = dims
    m, r = lax.axis_index("mode"), lax.axis_index("rank")
    CT = C * R
    K = D + B
    AB, FG = C * B, F * G

    def others(f):
        for mm_ in range(M):
            for rr_ in range(R):
                pl.when(jnp.logical_not((mm_ == m) & (rr_ == r)))(functools.partial(f, mm_, rr_))

    barrier = pltpu.get_barrier_semaphore()

    def greet(mm_, rr_):
        pl.semaphore_signal(barrier, inc=1, device_id={"mode": mm_, "rank": rr_}, device_id_type=MESH)

    others(greet)
    cp_s = pltpu.make_async_copy(s_hbm, s_all.at[r], loc_sem.at[0])
    cp_l = pltpu.make_async_copy(l_hbm, l_all.at[r], loc_sem.at[1])
    cp_o = pltpu.make_async_copy(op_hbm, op_raw, loc_sem.at[2])
    small = [
        pltpu.make_async_copy(src, dst, loc_sem.at[3 + k])
        for k, (src, dst) in enumerate(
            ((ri_hbm, ri_ref), (rl_hbm, rl_ref), (rc_hbm, rc_ref), (rr_hbm, rr_ref)))
    ]
    cp_s.start()
    cp_l.start()
    cp_o.start()
    for cp in small:
        cp.start()
    cp_s.wait()
    cp_l.wait()
    me = m * R + r
    gs = jnp.zeros((D, D), F32)
    for a2 in range(C // 2):
        e = jnp.concatenate([s_all[r, a * D:(a + 1) * D, :] for a in (2 * a2, 2 * a2 + 1)], axis=1)
        gs = gs + mm_nt(e, e)
    gs_all[me] = jnp.concatenate([gs, jnp.zeros((D, 128 - D), F32)], axis=1)
    pl.semaphore_wait(barrier, M * R - 1)

    def s_copy(rr_):
        return pltpu.make_async_remote_copy(
            src_ref=s_all.at[r], dst_ref=s_all.at[r], send_sem=s_send.at[rr_], recv_sem=s_recv.at[r],
            device_id={"rank": rr_}, device_id_type=MESH)

    def l_copy(rr_):
        return pltpu.make_async_remote_copy(
            src_ref=l_all.at[r], dst_ref=l_all.at[r], send_sem=l_send.at[rr_], recv_sem=l_recv.at[r],
            device_id={"rank": rr_}, device_id_type=MESH)

    def over_rank(f):
        for rr_ in range(R):
            pl.when(rr_ != r)(functools.partial(f, rr_))

    def start_sl(rr_):
        s_copy(rr_).start()
        l_copy(rr_).start()

    over_rank(start_sl)

    def sums(buf, send, recv):
        def copy(who, mm_, rr_):
            return pltpu.make_async_remote_copy(
                src_ref=buf.at[who], dst_ref=buf.at[who],
                send_sem=send.at[mm_ * R + rr_], recv_sem=recv.at[who],
                device_id={"mode": mm_, "rank": rr_}, device_id_type=MESH)

        def start():
            others(lambda mm_, rr_: copy(me, mm_, rr_).start())

        def finish():
            others(lambda mm_, rr_: copy(mm_ * R + rr_, mm_, rr_).wait_recv())
            total = buf[0]
            for who in range(1, M * R):
                total = total + buf[who]
            return total

        def sent():
            others(lambda mm_, rr_: copy(me, mm_, rr_).wait_send())

        return start, finish, sent

    gs_start, gs_finish, gs_sent = sums(gs_all, gs_send, gs_recv)
    g_start, g_finish, g_sent = sums(g_all, g_send, g_recv)
    gs_start()

    cp_o.wait()
    group = 2 * 128 // Y
    per = 256 // Y
    perm_op = turn(256, Y, per)

    def op_step(g, carry):
        both = jnp.concatenate(
            [op_raw[pl.ds(pl.multiple_of(g * 512, 512), 256), :],
             op_raw[pl.ds(pl.multiple_of(g * 512 + 256, 256), 256), :]], axis=1)
        out = mm(perm_op, both).astype(BF16)
        for h in range(2):
            for y in range(Y):
                op2[pl.ds(pl.multiple_of(g * 2 * per + h * per, per), per), y * J:(y + 1) * J] = (
                    out[y * per:(y + 1) * per, h * J:(h + 1) * J])
        return carry

    lax.fori_loop(0, X * I * Y // 512, op_step, 0, unroll=4)

    for cp in small:
        cp.wait()

    ri_t = ri_ref[...]
    perm_cb = turn(16 * B, B, 16)

    def project(rr_):
        for cg in range(C // 16):
            for c2 in range(8):
                c = cg * 16 + c2 * 2
                both = jnp.concatenate(
                    [s_all[rr_, c * D:(c + 1) * D, :], s_all[rr_, (c + 1) * D:(c + 2) * D, :]], axis=1)
                p = mm(ri_t, both).astype(BF16)
                for h in range(2):
                    for y in range(Y):
                        pblk[(c2 * 2 + h) * B:(c2 * 2 + h + 1) * B, y * J:(y + 1) * J] = (
                            p[y * B:(y + 1) * B, h * J:(h + 1) * J])
            zz = mm(perm_cb, pblk[...]).astype(BF16)
            for b in range(B):
                row = pl.multiple_of(b * CT + rr_ * C + cg * 16, 16)
                z_ref[pl.ds(row, 16), :] = zz[b * 16:(b + 1) * 16, :]

    project(r)

    def wait_sl(rr_):
        cp = s_copy(rr_)
        pltpu.make_async_remote_copy(
            src_ref=s_all.at[rr_], dst_ref=s_all.at[rr_], send_sem=s_send.at[rr_], recv_sem=s_recv.at[rr_],
            device_id={"rank": rr_}, device_id_type=MESH).wait_recv()
        pltpu.make_async_remote_copy(
            src_ref=l_all.at[rr_], dst_ref=l_all.at[rr_], send_sem=l_send.at[rr_], recv_sem=l_recv.at[rr_],
            device_id={"rank": rr_}, device_id_type=MESH).wait_recv()
        cp.wait_send()
        l_copy(rr_).wait_send()

    over_rank(wait_sl)
    for k in range(1, R):
        project(lax.rem(r + k, R))

    def main_step(x2, carry):
        w = op2[pl.ds(pl.multiple_of(x2 * 2 * I, 2 * I), 2 * I), :]
        a_ref[x2] = mm_nt(z_ref[...], w).astype(BF16)
        return carry

    lax.fori_loop(0, X // 2, main_step, 0, unroll=True)

    l2 = jnp.concatenate([l_all[rr_] for rr_ in range(R)], axis=0).astype(F32).T.astype(BF16)
    for b2 in range(B // 2):
        cols = []
        for h in range(2):
            b = b2 * 2 + h
            cols.append(jnp.concatenate(
                [a_ref[x // 2, b * CT + rr_ * C:b * CT + (rr_ + 1) * C, (x % 2) * I:(x % 2 + 1) * I]
                 for rr_ in range(R) for x in range(X)], axis=0))
        t = mm(l2, jnp.concatenate(cols, axis=1))
        for h in range(2):
            t_ref[pl.ds(b2 * 2 + h, A, stride=B), :] = t[:, h * I:(h + 1) * I]
    tb_ref[...] = t_ref[...].astype(BF16)

    local = m == r

    def t_copy(rr_):
        return pltpu.make_async_remote_copy(
            src_ref=tb_ref.at[pl.ds(rr_ * AB, AB)], dst_ref=t_recv.at[m],
            send_sem=t_send.at[rr_], recv_sem=t_rsem.at[m],
            device_id={"mode": r, "rank": rr_}, device_id_type=MESH)

    for rr_ in range(R):
        pl.when(jnp.logical_not(local & (rr_ == r)))(lambda rr_=rr_: t_copy(rr_).start())

    fac_ref[...] = eliminate(gs_finish(), D)

    row_ab, col_fg = iota((AB, 1), 0), iota((1, FG), 1)
    pick_a = one_hot(row_ab // B == iota((AB, C), 1))
    pick_b = one_hot(row_ab % B == iota((AB, B), 1))
    pick_f = one_hot(iota((F, FG), 0) == col_fg // G)
    pick_g = one_hot(iota((G, FG), 0) == col_fg % G)
    left = mm(mm_nt(pick_a, rl_ref[...]).astype(BF16), pick_f)
    right = mm(mm_nt(pick_b, rr_ref[...]).astype(BF16), pick_g)
    k_hi, k_lo = split2(left * right)
    rc = rc_ref[...]
    res_ref[...] = mm(k_hi, rc) + mm(k_lo, rc)

    @pl.when(local)
    def _():
        res_ref[...] -= t_ref[pl.ds(pl.multiple_of(r * AB, AB), AB), :]

    for mm_ in range(M):
        @pl.when(jnp.logical_not(local & (mm_ == m)))
        def _():
            pltpu.make_async_remote_copy(
                src_ref=tb_ref.at[pl.ds(0, AB)], dst_ref=t_recv.at[mm_],
                send_sem=t_send.at[0], recv_sem=t_rsem.at[mm_],
                device_id={"mode": r, "rank": 0}, device_id_type=MESH).wait_recv()
            res_ref[...] -= t_recv[mm_].astype(F32)

    hi, lo = split2(res_ref[...])
    g = jnp.zeros((2 * B, D + 2 * B), F32)
    for a2 in range(C // 2):
        hl = jnp.concatenate(
            [jnp.concatenate([hi[a * B:(a + 1) * B], lo[a * B:(a + 1) * B]], axis=0)
             for a in (2 * a2, 2 * a2 + 1)], axis=1)
        e = jnp.concatenate([s_all[r, a * D:(a + 1) * D, :] for a in (2 * a2, 2 * a2 + 1)], axis=1)
        g = g + mm_nt(hl, jnp.concatenate([e, hl], axis=0))
    g = g[:B] + g[B:]
    g_all[me] = jnp.concatenate([g[:, :D], g[:, D:K] + g[:, K:], jnp.zeros((B, 128 - K), F32)], axis=1)
    g_start()
    gram_ref[...] = g_finish()
    g_sent()
    gs_sent()
    for rr_ in range(R):
        pl.when(jnp.logical_not(local & (rr_ == r)))(lambda rr_=rr_: t_copy(rr_).wait_send())


def eliminate(gram, n):
    a = jnp.where(iota((n, 128), 1) == iota((n, 128), 0) + n, 1.0, gram)
    done = []
    for k in range(n):
        if k % 8 == 0 and k > 0:
            a = a[8:]
        ks = k % 8
        inv = lax.rsqrt(a[ks:ks + 1, k:k + 1])
        row = a[ks:ks + 1, :] * inv
        done.append(row)
        a = a - (a[:, k:k + 1] * inv) * row
    return jnp.concatenate(done, axis=0)


def factor_kernel(dims, s_hbm, res_ref, gram_ref, fac_ref, q_hbm, r_ref, s_ref, q_ref, sem, q_sem):
    M, R, C, D, J, X, I, Y, A, B, F, G = dims
    K = D + B
    cp = pltpu.make_async_copy(s_hbm, s_ref, sem)
    cp.start()
    exact = functools.partial(lax.dot_general, precision=lax.Precision.HIGHEST, preferred_element_type=F32)
    NN = (((1,), (0,)), ((), ()))
    u11, w11 = fac_ref[:, :D], fac_ref[:, D:2 * D]
    g21 = gram_ref[:, :D]
    l21 = exact(g21, w11, NT)
    u12 = exact(w11, g21, NT)
    s22 = gram_ref[:, D:K] - exact(l21, l21, NT)
    last = eliminate(jnp.concatenate([s22, jnp.zeros((B, 128 - B), F32)], axis=1), B)
    u22, w22 = last[:, :B], last[:, B:2 * B]
    w21 = -exact(w22, exact(l21, w11, NN), NN)
    upper = jnp.concatenate(
        [jnp.concatenate([u11, u12], axis=1), jnp.concatenate([jnp.zeros((B, D), F32), u22], axis=1)], axis=0)
    w = jnp.concatenate(
        [jnp.concatenate([w11, jnp.zeros((D, B), F32)], axis=1), jnp.concatenate([w21, w22], axis=1)], axis=0)
    tri = iota((K, K), 1) >= iota((K, K), 0)
    r_ref[...] = jnp.where(tri, upper, 0.0)
    w_hi, w_lo = split2(w)
    lhs = jnp.concatenate([w_hi, w_hi[:, D:], w_lo], axis=1)
    hi, lo = split2(res_ref[...])
    cp.wait()
    outs = []
    for a2 in range(C // 2):
        cols = []
        for a in (2 * a2, 2 * a2 + 1):
            s, h = s_ref[a * D:(a + 1) * D, :], hi[a * B:(a + 1) * B]
            cols.append(jnp.concatenate([s, h, lo[a * B:(a + 1) * B], s, h], axis=0))
        q = mm(lhs, jnp.concatenate(cols, axis=1))
        q_ref[2 * a2] = q[:, :I]
        q_ref[2 * a2 + 1] = q[:, I:]
        if (2 * a2 + 2) % 8 == 0:
            part = pl.ds(2 * a2 - 6, 8)
            out = pltpu.make_async_copy(q_ref.at[part], q_hbm.at[part], q_sem.at[a2 // 4])
            out.start()
            outs.append(out)
    for out in outs:
        out.wait()


def fused(n_mode, n_rank, solution_core, operator_core, left_interface, right_interface, rhs_left, rhs_core, rhs_right):
    C, J, D = solution_core.shape
    X, I, _, Y = operator_core.shape
    A = left_interface.shape[0]
    B = right_interface.shape[2]
    F, _, G = rhs_core.shape
    M, R = n_mode, n_rank
    dims = (M, R, C, D, J, X, I, Y, A, B, F, G)
    K = D + B
    s = solution_core.transpose(0, 2, 1).reshape(C * D, J)
    op = operator_core.transpose(0, 1, 3, 2).reshape(X * I * Y, J)
    li = left_interface.transpose(1, 2, 0).reshape(X * C, A)
    ri = right_interface.transpose(1, 2, 0).reshape(Y * B, D)
    rc = rhs_core.transpose(0, 2, 1).reshape(F * G, I)
    rl = rhs_left.T
    vmem = pl.BlockSpec(memory_space=pltpu.VMEM)
    hbm = pl.BlockSpec(memory_space=pl.ANY)
    DMA = pltpu.SemaphoreType.DMA
    res, gram, fac = pl.pallas_call(
        functools.partial(term_kernel, dims),
        out_shape=(jax.ShapeDtypeStruct((C * B, I), F32), jax.ShapeDtypeStruct((B, 128), F32),
                   jax.ShapeDtypeStruct((D, 128), F32)),
        in_specs=[hbm] * 7,
        out_specs=(vmem, vmem, vmem),
        scratch_shapes=[
            pltpu.VMEM(ri.shape, BF16),
            pltpu.VMEM(rl.shape, BF16),
            pltpu.VMEM(rc.shape, BF16),
            pltpu.VMEM(rhs_right.shape, BF16),
            pltpu.VMEM((R, C * D, J), BF16),
            pltpu.VMEM((R, X * C, A), BF16),
            pltpu.VMEM((X * I * Y, J), BF16),
            pltpu.VMEM((X * I, Y * J), BF16),
            pltpu.VMEM((16 * B, Y * J), BF16),
            pltpu.VMEM((B * C * R, Y * J), BF16),
            pltpu.VMEM((X // 2, B * C * R, 2 * I), BF16),
            pltpu.VMEM((A * B, I), F32),
            pltpu.VMEM((A * B, I), BF16),
            pltpu.VMEM((M, C * B, I), BF16),
            pltpu.VMEM((M * R, B, 128), F32),
            pltpu.VMEM((M * R, D, 128), F32),
            DMA((7,)), DMA((R,)), DMA((R,)), DMA((R,)), DMA((R,)),
            DMA((R,)), DMA((M,)), DMA((M * R,)), DMA((M * R,)), DMA((M * R,)), DMA((M * R,)),
        ],
        compiler_params=pltpu.CompilerParams(
            collective_id=0, has_side_effects=True, vmem_limit_bytes=62 * 1024 * 1024),
    )(s, op, li, ri, rl, rc, rhs_right)
    q, r_factor = pl.pallas_call(
        functools.partial(factor_kernel, dims),
        out_shape=(jax.ShapeDtypeStruct((C, K, I), F32), jax.ShapeDtypeStruct((K, K), F32)),
        in_specs=[hbm, vmem, vmem, vmem],
        out_specs=(hbm, vmem),
        scratch_shapes=[pltpu.VMEM(s.shape, BF16), pltpu.VMEM((C, K, I), F32), DMA, DMA((C // 8,))],
        compiler_params=pltpu.CompilerParams(vmem_limit_bytes=62 * 1024 * 1024),
    )(s, res, gram, fac)
    return q.transpose(0, 2, 1), r_factor


def plain(
    n_mode, n_rank, solution_core, operator_core, left_interface, right_interface, rhs_left, rhs_core, rhs_right
):
    highest = lax.Precision.HIGHEST
    left_rows, mode_rows, rank_full = solution_core.shape
    resid_rank = right_interface.shape[2]
    core_flat = solution_core.astype(F32).reshape(left_rows * mode_rows, rank_full)
    projected = jnp.einsum(
        "cjd,dyb->cjyb", solution_core, right_interface, preferred_element_type=F32
    ).astype(BF16)
    inter_turned = jnp.transpose(left_interface, (2, 1, 0))
    proj_piece = lax.all_gather(projected, "rank", axis=0, tiled=True)
    inter_piece = lax.all_gather(inter_turned, "rank", axis=0, tiled=True)
    applied = jnp.einsum(
        "xijy,cjyb->cxib", operator_core, proj_piece, preferred_element_type=F32
    ).astype(BF16)
    partial_value = jnp.einsum("cxa,cxib->aib", inter_piece, applied, preferred_element_type=F32)
    turned = lax.all_to_all(partial_value, "rank", split_axis=0, concat_axis=1, tiled=True)
    summed = lax.psum_scatter(turned, "mode", scatter_dimension=1, tiled=True)
    rhs_term = jnp.einsum(
        "af,fig,gb->aib",
        rhs_left.astype(F32),
        rhs_core.astype(F32),
        rhs_right.astype(F32),
        precision=highest,
    )
    residual_core = rhs_term - summed
    resid_flat = residual_core.reshape(left_rows * mode_rows, resid_rank)
    enriched = jnp.concatenate([core_flat, resid_flat], axis=1)
    gram = lax.psum(jnp.dot(enriched.T, enriched, precision=highest), ("mode", "rank"))
    lower = jnp.linalg.cholesky(gram)
    solved = lax.linalg.triangular_solve(
        lower, enriched, left_side=False, lower=True, transpose_a=True
    )
    q_core = solved.reshape(left_rows, mode_rows, rank_full + resid_rank)
    return (q_core, lower.T)


def per_device(n_mode, n_rank, *args):
    solution_core, operator_core, _, right_interface, _, rhs_core, _ = args
    C, J, D = solution_core.shape
    X, I, _, Y = operator_core.shape
    B = right_interface.shape[2]
    tiles = (
        n_mode == n_rank and J == 128 and I == 128 and rhs_core.shape[1] == I
        and C % 16 == 0 and B == 16 and D % 16 == 0 and D + B <= 128 and 2 * D <= 128
        and 256 % Y == 0 and (256 // Y) % 16 == 0 and X % 2 == 0
    )
    return (fused if tiles else plain)(n_mode, n_rank, *args)


def solution(mesh):
    in_specs = (
        P(("sys", "rank"), "mode", None),
        P("sys", "rank", "mode", None),
        P("sys", None, "rank"),
        P("sys", None, None),
        P(("sys", "rank"), None),
        P("sys", "mode", None),
        P("sys", None),
    )
    out_specs = (P(("sys", "rank"), "mode", None), P("sys", None))
    return jax.shard_map(
        functools.partial(per_device, mesh.shape["mode"], mesh.shape["rank"]),
        mesh=mesh, in_specs=in_specs, out_specs=out_specs, check_vma=False,
    )
```

```python
import functools

import jax
import jax.numpy as jnp
from jax import lax
from jax.experimental import pallas as pl
from jax.experimental.pallas import tpu as pltpu
from jax.sharding import PartitionSpec as P

F32 = jnp.float32
BF16 = jnp.bfloat16
MESH = pl.DeviceIdType.MESH
NT = (((1,), (1,)), ((), ()))


def mm(a, b):
    return jnp.dot(a, b, preferred_element_type=F32)


def mm_nt(a, b):
    return lax.dot_general(a, b, NT, preferred_element_type=F32)


def iota(shape, dim):
    return lax.broadcasted_iota(jnp.int32, shape, dim)


def one_hot(cond):
    return jnp.where(cond, 1.0, 0.0).astype(BF16)


def turn(rows, inner, outer):
    row, col = iota((rows, rows), 0), iota((rows, rows), 1)
    return one_hot(col == (row % outer) * inner + row // outer)


def split2(x):
    hi = x.astype(BF16)
    return hi, (x - hi.astype(F32)).astype(BF16)


def term_kernel(
    dims,
    s_hbm, op_hbm, l_hbm, ri_hbm, rl_hbm, rc_hbm, rr_hbm,
    res_ref, gram_ref, fac_ref,
    ri_ref, rl_ref, rc_ref, rr_ref, s_all, l_all, op_raw, op2, pblk, z_ref, a_ref, t_ref, tb_ref, t_recv, g_all, gs_all,
    loc_sem, s_send, s_recv, l_send, l_recv, t_send, t_rsem, g_send, g_recv, gs_send, gs_recv,
):
    M, R, C, D, J, X, I, Y, A, B, F, G = dims
    m, r = lax.axis_index("mode"), lax.axis_index("rank")
    CT = C * R
    K = D + B
    AB, FG = C * B, F * G

    def others(f):
        for mm_ in range(M):
            for rr_ in range(R):
                pl.when(jnp.logical_not((mm_ == m) & (rr_ == r)))(functools.partial(f, mm_, rr_))

    barrier = pltpu.get_barrier_semaphore()

    def greet(mm_, rr_):
        pl.semaphore_signal(barrier, inc=1, device_id={"mode": mm_, "rank": rr_}, device_id_type=MESH)

    others(greet)
    cp_s = pltpu.make_async_copy(s_hbm, s_all.at[r], loc_sem.at[0])
    cp_l = pltpu.make_async_copy(l_hbm, l_all.at[r], loc_sem.at[1])
    cp_o = pltpu.make_async_copy(op_hbm, op_raw, loc_sem.at[2])
    small = [
        pltpu.make_async_copy(src, dst, loc_sem.at[3 + k])
        for k, (src, dst) in enumerate(
            ((ri_hbm, ri_ref), (rl_hbm, rl_ref), (rc_hbm, rc_ref), (rr_hbm, rr_ref)))
    ]
    cp_s.start()
    cp_l.start()
    cp_o.start()
    for cp in small:
        cp.start()
    cp_s.wait()
    cp_l.wait()
    me = m * R + r
    gs = jnp.zeros((D, D), F32)
    for a2 in range(C // 2):
        e = jnp.concatenate([s_all[r, a * D:(a + 1) * D, :] for a in (2 * a2, 2 * a2 + 1)], axis=1)
        gs = gs + mm_nt(e, e)
    gs_all[me] = jnp.concatenate([gs, jnp.zeros((D, 128 - D), F32)], axis=1)
    pl.semaphore_wait(barrier, M * R - 1)

    def s_copy(rr_):
        return pltpu.make_async_remote_copy(
            src_ref=s_all.at[r], dst_ref=s_all.at[r], send_sem=s_send.at[rr_], recv_sem=s_recv.at[r],
            device_id={"rank": rr_}, device_id_type=MESH)

    def l_copy(rr_):
        return pltpu.make_async_remote_copy(
            src_ref=l_all.at[r], dst_ref=l_all.at[r], send_sem=l_send.at[rr_], recv_sem=l_recv.at[r],
            device_id={"rank": rr_}, device_id_type=MESH)

    def over_rank(f):
        for rr_ in range(R):
            pl.when(rr_ != r)(functools.partial(f, rr_))

    def start_sl(rr_):
        s_copy(rr_).start()
        l_copy(rr_).start()

    over_rank(start_sl)

    def sums(buf, send, recv):
        def copy(who, mm_, rr_):
            return pltpu.make_async_remote_copy(
                src_ref=buf.at[who], dst_ref=buf.at[who],
                send_sem=send.at[mm_ * R + rr_], recv_sem=recv.at[who],
                device_id={"mode": mm_, "rank": rr_}, device_id_type=MESH)

        def start():
            others(lambda mm_, rr_: copy(me, mm_, rr_).start())

        def finish():
            others(lambda mm_, rr_: copy(mm_ * R + rr_, mm_, rr_).wait_recv())
            total = buf[0]
            for who in range(1, M * R):
                total = total + buf[who]
            return total

        def sent():
            others(lambda mm_, rr_: copy(me, mm_, rr_).wait_send())

        return start, finish, sent

    gs_start, gs_finish, gs_sent = sums(gs_all, gs_send, gs_recv)
    g_start, g_finish, g_sent = sums(g_all, g_send, g_recv)
    gs_start()

    cp_o.wait()
    group = 2 * 128 // Y
    per = 256 // Y
    perm_op = turn(256, Y, per)

    def op_step(g, carry):
        both = jnp.concatenate(
            [op_raw[pl.ds(pl.multiple_of(g * 512, 512), 256), :],
             op_raw[pl.ds(pl.multiple_of(g * 512 + 256, 256), 256), :]], axis=1)
        out = mm(perm_op, both).astype(BF16)
        for h in range(2):
            for y in range(Y):
                op2[pl.ds(pl.multiple_of(g * 2 * per + h * per, per), per), y * J:(y + 1) * J] = (
                    out[y * per:(y + 1) * per, h * J:(h + 1) * J])
        return carry

    lax.fori_loop(0, X * I * Y // 512, op_step, 0, unroll=True)

    for cp in small:
        cp.wait()

    ri_t = ri_ref[...]
    perm_cb = turn(16 * B, B, 16)

    def project(rr_):
        for cg in range(C // 16):
            for c2 in range(8):
                c = cg * 16 + c2 * 2
                both = jnp.concatenate(
                    [s_all[rr_, c * D:(c + 1) * D, :], s_all[rr_, (c + 1) * D:(c + 2) * D, :]], axis=1)
                p = mm(ri_t, both).astype(BF16)
                for h in range(2):
                    for y in range(Y):
                        pblk[(c2 * 2 + h) * B:(c2 * 2 + h + 1) * B, y * J:(y + 1) * J] = (
                            p[y * B:(y + 1) * B, h * J:(h + 1) * J])
            zz = mm(perm_cb, pblk[...]).astype(BF16)
            for b in range(B):
                row = pl.multiple_of(b * CT + rr_ * C + cg * 16, 16)
                z_ref[pl.ds(row, 16), :] = zz[b * 16:(b + 1) * 16, :]

    project(r)

    def wait_sl(rr_):
        cp = s_copy(rr_)
        pltpu.make_async_remote_copy(
            src_ref=s_all.at[rr_], dst_ref=s_all.at[rr_], send_sem=s_send.at[rr_], recv_sem=s_recv.at[rr_],
            device_id={"rank": rr_}, device_id_type=MESH).wait_recv()
        pltpu.make_async_remote_copy(
            src_ref=l_all.at[rr_], dst_ref=l_all.at[rr_], send_sem=l_send.at[rr_], recv_sem=l_recv.at[rr_],
            device_id={"rank": rr_}, device_id_type=MESH).wait_recv()
        cp.wait_send()
        l_copy(rr_).wait_send()

    over_rank(wait_sl)
    for k in range(1, R):
        project(lax.rem(r + k, R))

    def main_step(x2, carry):
        w = op2[pl.ds(pl.multiple_of(x2 * 2 * I, 2 * I), 2 * I), :]
        a_ref[x2] = mm_nt(z_ref[...], w).astype(BF16)
        return carry

    lax.fori_loop(0, X // 2, main_step, 0, unroll=True)

    l2 = jnp.concatenate([l_all[rr_] for rr_ in range(R)], axis=0).astype(F32).T.astype(BF16)
    for b2 in range(B // 2):
        cols = []
        for h in range(2):
            b = b2 * 2 + h
            cols.append(jnp.concatenate(
                [a_ref[x // 2, b * CT + rr_ * C:b * CT + (rr_ + 1) * C, (x % 2) * I:(x % 2 + 1) * I]
                 for rr_ in range(R) for x in range(X)], axis=0))
        t = mm(l2, jnp.concatenate(cols, axis=1))
        for h in range(2):
            t_ref[pl.ds(b2 * 2 + h, A, stride=B), :] = t[:, h * I:(h + 1) * I]
    tb_ref[...] = t_ref[...].astype(BF16)

    local = m == r

    def t_copy(rr_):
        return pltpu.make_async_remote_copy(
            src_ref=tb_ref.at[pl.ds(rr_ * AB, AB)], dst_ref=t_recv.at[m],
            send_sem=t_send.at[rr_], recv_sem=t_rsem.at[m],
            device_id={"mode": r, "rank": rr_}, device_id_type=MESH)

    for rr_ in range(R):
        pl.when(jnp.logical_not(local & (rr_ == r)))(lambda rr_=rr_: t_copy(rr_).start())

    fac_ref[...] = eliminate(gs_finish(), D)

    row_ab, col_fg = iota((AB, 1), 0), iota((1, FG), 1)
    pick_a = one_hot(row_ab // B == iota((AB, C), 1))
    pick_b = one_hot(row_ab % B == iota((AB, B), 1))
    pick_f = one_hot(iota((F, FG), 0) == col_fg // G)
    pick_g = one_hot(iota((G, FG), 0) == col_fg % G)
    left = mm(mm_nt(pick_a, rl_ref[...]).astype(BF16), pick_f)
    right = mm(mm_nt(pick_b, rr_ref[...]).astype(BF16), pick_g)
    k_hi, k_lo = split2(left * right)
    rc = rc_ref[...]
    res_ref[...] = mm(k_hi, rc) + mm(k_lo, rc)

    @pl.when(local)
    def _():
        res_ref[...] -= t_ref[pl.ds(pl.multiple_of(r * AB, AB), AB), :]

    for mm_ in range(M):
        @pl.when(jnp.logical_not(local & (mm_ == m)))
        def _():
            pltpu.make_async_remote_copy(
                src_ref=tb_ref.at[pl.ds(0, AB)], dst_ref=t_recv.at[mm_],
                send_sem=t_send.at[0], recv_sem=t_rsem.at[mm_],
                device_id={"mode": r, "rank": 0}, device_id_type=MESH).wait_recv()
            res_ref[...] -= t_recv[mm_].astype(F32)

    hi, lo = split2(res_ref[...])
    g = jnp.zeros((2 * B, D + 2 * B), F32)
    for a2 in range(C // 2):
        hl = jnp.concatenate(
            [jnp.concatenate([hi[a * B:(a + 1) * B], lo[a * B:(a + 1) * B]], axis=0)
             for a in (2 * a2, 2 * a2 + 1)], axis=1)
        e = jnp.concatenate([s_all[r, a * D:(a + 1) * D, :] for a in (2 * a2, 2 * a2 + 1)], axis=1)
        g = g + mm_nt(hl, jnp.concatenate([e, hl], axis=0))
    g = g[:B] + g[B:]
    g_all[me] = jnp.concatenate([g[:, :D], g[:, D:K] + g[:, K:], jnp.zeros((B, 128 - K), F32)], axis=1)
    g_start()
    gram_ref[...] = g_finish()
    g_sent()
    gs_sent()
    for rr_ in range(R):
        pl.when(jnp.logical_not(local & (rr_ == r)))(lambda rr_=rr_: t_copy(rr_).wait_send())


def eliminate(gram, n):
    a = jnp.where(iota((n, 128), 1) == iota((n, 128), 0) + n, 1.0, gram)
    done = []
    for k in range(n):
        if k % 8 == 0 and k > 0:
            a = a[8:]
        ks = k % 8
        inv = lax.rsqrt(a[ks:ks + 1, k:k + 1])
        row = a[ks:ks + 1, :] * inv
        done.append(row)
        a = a - (a[:, k:k + 1] * inv) * row
    return jnp.concatenate(done, axis=0)


def factor_kernel(dims, s_hbm, res_ref, gram_ref, fac_ref, q_hbm, r_ref, s_ref, q_ref, sem, q_sem):
    M, R, C, D, J, X, I, Y, A, B, F, G = dims
    K = D + B
    cp = pltpu.make_async_copy(s_hbm, s_ref, sem)
    cp.start()
    exact = functools.partial(lax.dot_general, precision=lax.Precision.HIGHEST, preferred_element_type=F32)
    NN = (((1,), (0,)), ((), ()))
    u11, w11 = fac_ref[:, :D], fac_ref[:, D:2 * D]
    g21 = gram_ref[:, :D]
    l21 = exact(g21, w11, NT)
    u12 = exact(w11, g21, NT)
    s22 = gram_ref[:, D:K] - exact(l21, l21, NT)
    last = eliminate(jnp.concatenate([s22, jnp.zeros((B, 128 - B), F32)], axis=1), B)
    u22, w22 = last[:, :B], last[:, B:2 * B]
    w21 = -exact(w22, exact(l21, w11, NN), NN)
    upper = jnp.concatenate(
        [jnp.concatenate([u11, u12], axis=1), jnp.concatenate([jnp.zeros((B, D), F32), u22], axis=1)], axis=0)
    w = jnp.concatenate(
        [jnp.concatenate([w11, jnp.zeros((D, B), F32)], axis=1), jnp.concatenate([w21, w22], axis=1)], axis=0)
    tri = iota((K, K), 1) >= iota((K, K), 0)
    r_ref[...] = jnp.where(tri, upper, 0.0)
    w_hi, w_lo = split2(w)
    lhs = jnp.concatenate([w_hi, w_hi[:, D:], w_lo], axis=1)
    hi, lo = split2(res_ref[...])
    cp.wait()
    outs = []
    for a2 in range(C // 2):
        cols = []
        for a in (2 * a2, 2 * a2 + 1):
            s, h = s_ref[a * D:(a + 1) * D, :], hi[a * B:(a + 1) * B]
            cols.append(jnp.concatenate([s, h, lo[a * B:(a + 1) * B], s, h], axis=0))
        q = mm(lhs, jnp.concatenate(cols, axis=1))
        q_ref[2 * a2] = q[:, :I]
        q_ref[2 * a2 + 1] = q[:, I:]
        if (2 * a2 + 2) % 8 == 0:
            part = pl.ds(2 * a2 - 6, 8)
            out = pltpu.make_async_copy(q_ref.at[part], q_hbm.at[part], q_sem.at[a2 // 4])
            out.start()
            outs.append(out)
    for out in outs:
        out.wait()


def fused(n_mode, n_rank, solution_core, operator_core, left_interface, right_interface, rhs_left, rhs_core, rhs_right):
    C, J, D = solution_core.shape
    X, I, _, Y = operator_core.shape
    A = left_interface.shape[0]
    B = right_interface.shape[2]
    F, _, G = rhs_core.shape
    M, R = n_mode, n_rank
    dims = (M, R, C, D, J, X, I, Y, A, B, F, G)
    K = D + B
    s = solution_core.transpose(0, 2, 1).reshape(C * D, J)
    op = operator_core.transpose(0, 1, 3, 2).reshape(X * I * Y, J)
    li = left_interface.transpose(1, 2, 0).reshape(X * C, A)
    ri = right_interface.transpose(1, 2, 0).reshape(Y * B, D)
    rc = rhs_core.transpose(0, 2, 1).reshape(F * G, I)
    rl = rhs_left.T
    vmem = pl.BlockSpec(memory_space=pltpu.VMEM)
    hbm = pl.BlockSpec(memory_space=pl.ANY)
    DMA = pltpu.SemaphoreType.DMA
    res, gram, fac = pl.pallas_call(
        functools.partial(term_kernel, dims),
        out_shape=(jax.ShapeDtypeStruct((C * B, I), F32), jax.ShapeDtypeStruct((B, 128), F32),
                   jax.ShapeDtypeStruct((D, 128), F32)),
        in_specs=[hbm] * 7,
        out_specs=(vmem, vmem, vmem),
        scratch_shapes=[
            pltpu.VMEM(ri.shape, BF16),
            pltpu.VMEM(rl.shape, BF16),
            pltpu.VMEM(rc.shape, BF16),
            pltpu.VMEM(rhs_right.shape, BF16),
            pltpu.VMEM((R, C * D, J), BF16),
            pltpu.VMEM((R, X * C, A), BF16),
            pltpu.VMEM((X * I * Y, J), BF16),
            pltpu.VMEM((X * I, Y * J), BF16),
            pltpu.VMEM((16 * B, Y * J), BF16),
            pltpu.VMEM((B * C * R, Y * J), BF16),
            pltpu.VMEM((X // 2, B * C * R, 2 * I), BF16),
            pltpu.VMEM((A * B, I), F32),
            pltpu.VMEM((A * B, I), BF16),
            pltpu.VMEM((M, C * B, I), BF16),
            pltpu.VMEM((M * R, B, 128), F32),
            pltpu.VMEM((M * R, D, 128), F32),
            DMA((7,)), DMA((R,)), DMA((R,)), DMA((R,)), DMA((R,)),
            DMA((R,)), DMA((M,)), DMA((M * R,)), DMA((M * R,)), DMA((M * R,)), DMA((M * R,)),
        ],
        compiler_params=pltpu.CompilerParams(
            collective_id=0, has_side_effects=True, vmem_limit_bytes=62 * 1024 * 1024),
    )(s, op, li, ri, rl, rc, rhs_right)
    q, r_factor = pl.pallas_call(
        functools.partial(factor_kernel, dims),
        out_shape=(jax.ShapeDtypeStruct((C, K, I), F32), jax.ShapeDtypeStruct((K, K), F32)),
        in_specs=[hbm, vmem, vmem, vmem],
        out_specs=(hbm, vmem),
        scratch_shapes=[pltpu.VMEM(s.shape, BF16), pltpu.VMEM((C, K, I), F32), DMA, DMA((C // 8,))],
        compiler_params=pltpu.CompilerParams(vmem_limit_bytes=62 * 1024 * 1024),
    )(s, res, gram, fac)
    return q.transpose(0, 2, 1), r_factor


def plain(
    n_mode, n_rank, solution_core, operator_core, left_interface, right_interface, rhs_left, rhs_core, rhs_right
):
    highest = lax.Precision.HIGHEST
    left_rows, mode_rows, rank_full = solution_core.shape
    resid_rank = right_interface.shape[2]
    core_flat = solution_core.astype(F32).reshape(left_rows * mode_rows, rank_full)
    projected = jnp.einsum(
        "cjd,dyb->cjyb", solution_core, right_interface, preferred_element_type=F32
    ).astype(BF16)
    inter_turned = jnp.transpose(left_interface, (2, 1, 0))
    proj_piece = lax.all_gather(projected, "rank", axis=0, tiled=True)
    inter_piece = lax.all_gather(inter_turned, "rank", axis=0, tiled=True)
    applied = jnp.einsum(
        "xijy,cjyb->cxib", operator_core, proj_piece, preferred_element_type=F32
    ).astype(BF16)
    partial_value = jnp.einsum("cxa,cxib->aib", inter_piece, applied, preferred_element_type=F32)
    turned = lax.all_to_all(partial_value, "rank", split_axis=0, concat_axis=1, tiled=True)
    summed = lax.psum_scatter(turned, "mode", scatter_dimension=1, tiled=True)
    rhs_term = jnp.einsum(
        "af,fig,gb->aib",
        rhs_left.astype(F32),
        rhs_core.astype(F32),
        rhs_right.astype(F32),
        precision=highest,
    )
    residual_core = rhs_term - summed
    resid_flat = residual_core.reshape(left_rows * mode_rows, resid_rank)
    enriched = jnp.concatenate([core_flat, resid_flat], axis=1)
    gram = lax.psum(jnp.dot(enriched.T, enriched, precision=highest), ("mode", "rank"))
    lower = jnp.linalg.cholesky(gram)
    solved = lax.linalg.triangular_solve(
        lower, enriched, left_side=False, lower=True, transpose_a=True
    )
    q_core = solved.reshape(left_rows, mode_rows, rank_full + resid_rank)
    return (q_core, lower.T)


def per_device(n_mode, n_rank, *args):
    solution_core, operator_core, _, right_interface, _, rhs_core, _ = args
    C, J, D = solution_core.shape
    X, I, _, Y = operator_core.shape
    B = right_interface.shape[2]
    tiles = (
        n_mode == n_rank and J == 128 and I == 128 and rhs_core.shape[1] == I
        and C % 16 == 0 and B == 16 and D % 16 == 0 and D + B <= 128 and 2 * D <= 128
        and 256 % Y == 0 and (256 // Y) % 16 == 0 and X % 2 == 0
    )
    return (fused if tiles else plain)(n_mode, n_rank, *args)


def solution(mesh):
    in_specs = (
        P(("sys", "rank"), "mode", None),
        P("sys", "rank", "mode", None),
        P("sys", None, "rank"),
        P("sys", None, None),
        P(("sys", "rank"), None),
        P("sys", "mode", None),
        P("sys", None),
    )
    out_specs = (P(("sys", "rank"), "mode", None), P("sys", None))
    return jax.shard_map(
        functools.partial(per_device, mesh.shape["mode"], mesh.shape["rank"]),
        mesh=mesh, in_specs=in_specs, out_specs=out_specs, check_vma=False,
    )
```
